128 devices in a mesh: box: 16 (over x, y), bal: 8 (over z, core).
Axes of the slice: x: 4, y: 4, z: 4, core: 2. Of those that a mesh axis runs over, the one named last changes fastest.
Arguments:
- species_state: bfloat16 [512, 218, 1024], P('box', None, 'bal'), may hold values from -6 to 6
- stiffness: int32 [512, 8], P('box', 'bal'), may hold values from 6 to 12
- send_list: int32 [16, 8, 16, 4], P('box', 'bal'), may hold values from -1 to 31, as said below
- jacobian: bfloat16 [1024, 8, 256, 256], P('box', 'bal'), may hold values from -0.375 to 0.375
- pattern: int32 [1024, 8, 4, 4], P('box', 'bal'), may hold values 0 or 1
- diffusivity: float32 [218], replicated, may hold values from 0.02 to 0.24
Outputs:
- species_field: float32 [512, 218, 1024], P('box', None, 'bal')
The draws below stay inside these ranges and needn't reach their ends.
Inputs may be any that keep to these rules, and one draw needn't show every extreme that they name: `send_list`: in the table of device (b, j), entry (o, c) is the local tile that goes to slot c of owner o in the same j, or -1 for an empty slot. Every local tile stands exactly once in its device's table. In every j, one owner has all 4 slots from every device filled. Any slot of the other owners may be filled or empty.
All inputs are finite; a program needn't handle non-finite values. No bound on the sum of `pattern` on one device may be relied on, other than what follows from the above.
Results may differ from the reference program's by a relative error of at most 0.0003.
Values may be sent and summed in bfloat16 or wider, within the bound.
No kernel may reach another device: no remote copies, remote signals or barrier semaphores. Data moves between devices by JAX's collectives and lax.ppermute only.
A program may use at most 128 MiB of HBM per device.

```python
import math
import jax
import jax.numpy as jnp
from jax import lax

S = 218
BL = 64
TD = 32
KMAX = 12
DSTEPS = 2
NB = 4
SP = 256
C = 4
NX = 512
NY = 1024
OWN_SLOTS = 1024
N_BOX = 16
N_BAL = 8


def relayout_plan(key):
    key_level = jax.random.fold_in(key, 101)
    key_extra = jax.random.fold_in(key, 102)
    key_owner = jax.random.fold_in(key, 103)
    key_order = jax.random.fold_in(key, 104)
    key_slots = jax.random.fold_in(key, 105)
    key_favour = jax.random.fold_in(key, 106)
    stiff_level = jax.random.randint(key_level, (N_BOX, N_BAL, 1), 0, KMAX // 2 + 1)
    extra_turns = jax.random.randint(key_extra, (N_BOX, N_BAL, TD), 0, KMAX // 2 + 1)
    counts = KMAX // 2 + jnp.minimum(extra_turns, stiff_level)
    tile_pos = jnp.arange(TD)[None, None, :]
    first_box = (jnp.arange(N_BOX) == 0)[:, None, None] & (jnp.arange(N_BAL) == 0)[None, :, None]
    counts = jnp.where(first_box & (tile_pos == 0), KMAX, counts)
    counts = jnp.where(first_box & (tile_pos == 1), KMAX // 2, counts)
    owner_pick = jax.random.randint(key_owner, (N_BAL,), 0, N_BOX)
    rank_score = counts * (65536 * TD) + jax.random.randint(key_order, (N_BOX, N_BAL, TD), 0, 65536) * TD + tile_pos
    light_order = jnp.argsort(rank_score, axis=-1, stable=True).astype(jnp.int32)
    others = N_BOX - 1
    other_slots = others * C
    slot_scores = jax.random.randint(key_slots, (N_BOX, N_BAL, other_slots), 0, 65536).astype(jnp.int32)
    favoured = jax.random.randint(key_favour, (N_BOX, N_BAL), 0, 2 * others).astype(jnp.int32)

    def fill(order_row, owner, score_row, favour_no):
        lightest = order_row[:C]
        remaining = order_row[C:]
        flat_no = jnp.arange(other_slots, dtype=jnp.int32)
        other_no = flat_no // C
        slot_no = flat_no % C
        owner_no = other_no + (other_no >= owner).astype(jnp.int32)
        later = (other_no != favour_no).astype(jnp.int32)
        full_score = later * (65536 * other_slots) + score_row * other_slots + flat_no
        chosen = jnp.argsort(full_score, stable=True).astype(jnp.int32)[:TD - C]
        flat_slots = jnp.concatenate([owner * C + jnp.arange(C, dtype=jnp.int32), owner_no[chosen] * C + slot_no[chosen]])
        table_row = jnp.full((N_BOX * C,), -1, jnp.int32).at[flat_slots].set(jnp.concatenate([lightest, remaining]).astype(jnp.int32))
        return table_row.reshape(N_BOX, C)
    owners_full = jnp.broadcast_to(owner_pick[None, :], (N_BOX, N_BAL)).astype(jnp.int32)
    tables = jax.vmap(jax.vmap(fill))(light_order, owners_full, slot_scores, favoured)
    return (counts.astype(jnp.int32), tables)


def draw_stiffness(key, part):
    counts, tables = relayout_plan(key)
    return counts.transpose(0, 2, 1).reshape(N_BOX * TD, N_BAL)


def draw_send_list(key, part):
    counts, tables = relayout_plan(key)
    return tables


def with_ends(values, rng, smallest, largest):
    extent = values.shape
    place = [jax.random.randint(jax.random.fold_in(rng, axis), (), 0, extent[axis]) for axis in range(len(extent))]
    values = values.at[tuple(place)].set(smallest)
    longest = extent.index(max(extent))
    place[longest] = (place[longest] + 1) % extent[longest]
    return values.at[tuple(place)].set(largest)


def steps_of(own_key, shape, split, low, top_value):
    gain, own = 1.0, jax.random.fold_in(own_key, 6)
    for dim, parts in split:
        heights = jnp.exp(jax.random.uniform(jax.random.fold_in(own, dim), (parts,), jnp.float32, low / len(split), top_value / len(split)))
        gain = gain * jnp.repeat(heights, shape[dim] // parts).reshape([-1 if axis == dim else 1 for axis in range(len(shape))])
    return gain


def gaussian(stream_key, shape, spread, reach, shards=(), held_as=jnp.bfloat16):
    result = spread * jax.random.normal(stream_key, shape, jnp.float32)
    if shards:
        result = result * steps_of(stream_key, shape, shards, -0.22, 0.18)
    return jnp.clip(result, -reach, reach).astype(held_as)


def setup_inputs(seed: int = 0) -> dict:
    key_list = jax.random.split(jax.random.key(seed), 7)
    species_state = gaussian(key_list[0], (NX, S, NY), 1.0, 6.0, ((0, 16), (2, 8)))
    stiffness = draw_stiffness(jax.random.fold_in(key_list[6], 71), 0)
    send_list = draw_send_list(jax.random.fold_in(key_list[6], 71), 0)
    jacobian = gaussian(key_list[3], (OWN_SLOTS, N_BAL, SP, SP), SP ** -0.5, 0.375, ((0, 16), (1, 8)))
    pattern = with_ends((jax.random.randint(key_list[4], (OWN_SLOTS, N_BAL, NB, NB), 0, 4) < 3).astype(jnp.int32), jax.random.fold_in(key_list[4], 1), 0, 1)
    diffusivity = jnp.clip(jnp.exp(jax.random.uniform(key_list[5], (S,), jnp.float32, math.log(0.02), math.log(0.24))), 0.02, 0.24)
    return dict(species_state=species_state, stiffness=stiffness, send_list=send_list, jacobian=jacobian, pattern=pattern, diffusivity=diffusivity)


epsilon = 1e-6


def masked_operator(jac_block, blocks):
    expanded = jnp.repeat(jnp.repeat(blocks.astype(jnp.float32), BL, axis=-2), BL, axis=-1)
    inside = (jnp.arange(SP) < S).astype(jnp.float32)
    return jac_block.astype(jnp.float32) * expanded * inside[:, None] * inside[None, :]


def solve_tile(tile_data, operator, count):
    start_value = jnp.pad(tile_data.astype(jnp.float32), ((0, SP - S), (0, 0)))
    remainder = jnp.dot(operator, start_value, precision=lax.Precision.HIGHEST)

    def advance(turn_no, state_pair):
        guess, left_over = state_pair
        mapped = left_over - jnp.dot(operator, left_over, precision=lax.Precision.HIGHEST)
        step_size = jnp.sum(left_over * mapped, axis=0) / (jnp.sum(mapped * mapped, axis=0) + epsilon)
        return guess + step_size * left_over, left_over - step_size * mapped

    guess, left_over = lax.fori_loop(0, count, advance, (start_value, remainder))
    return guess[:S]


def reference(species_state, stiffness, send_list, jacobian, pattern, diffusivity):
    box_count = send_list.shape[0]
    groups = send_list.shape[1]
    slots_cap = send_list.shape[3]
    tiles_dev = stiffness.shape[0] // box_count
    slots_dev = jacobian.shape[0] // box_count
    tile_width = species_state.shape[2] // groups
    flat_table = send_list.reshape(box_count, groups, box_count * slots_cap)

    def inverse(table_row):
        target = jnp.where(table_row >= 0, table_row, tiles_dev).astype(jnp.int32)
        return jnp.zeros((tiles_dev,), jnp.int32).at[target].set(
            jnp.arange(box_count * slots_cap, dtype=jnp.int32), mode="drop")

    slot_of = jax.vmap(jax.vmap(inverse))(flat_table)

    def one_tile(flat_index):
        home_box = flat_index // (groups * tiles_dev)
        group_no = (flat_index // tiles_dev) % groups
        tile_no = flat_index % tiles_dev
        flat_slot = slot_of[home_box, group_no, tile_no]
        owner_no = flat_slot // slots_cap
        slot_no = flat_slot % slots_cap
        jac_row = (owner_no * slots_dev + home_box * slots_cap + slot_no).astype(jnp.int32)
        grid_row = (home_box * tiles_dev + tile_no).astype(jnp.int32)
        tile_data = lax.dynamic_slice(
            species_state, (grid_row, jnp.int32(0), (group_no * tile_width).astype(jnp.int32)),
            (1, S, tile_width))[0]
        operator = masked_operator(jacobian[jac_row, group_no], pattern[jac_row, group_no])
        return solve_tile(tile_data, operator, stiffness[grid_row, group_no])

    solved = lax.map(one_tile, jnp.arange(box_count * groups * tiles_dev, dtype=jnp.int32))
    reacted = solved.reshape(box_count, groups, tiles_dev, S, tile_width)
    reacted = reacted.transpose(0, 2, 3, 1, 4).reshape(box_count * tiles_dev, S, groups * tile_width)
    diffuse_rate = diffusivity[None, :, None]
    species_field = reacted
    for repeat_no in range(DSTEPS):
        padded = jnp.pad(species_field, ((1, 1), (0, 0), (1, 1)))
        neighbours = padded[2:, :, 1:-1] + padded[:-2, :, 1:-1] + padded[1:-1, :, 2:] + padded[1:-1, :, :-2]
        species_field = species_field + diffuse_rate * (neighbours - 4.0 * species_field)
    return species_field
```

```python
import functools

import jax
import jax.numpy as jnp
from jax import lax
from jax.experimental import pallas as pl
from jax.experimental.pallas import tpu as pltpu
from jax.sharding import PartitionSpec as P

S = 218
SR = 224
SP = 256
BL = 64
NB = 4
PACK = 400
LANES = 128
EPSILON = 1e-06
GROUP = 4
CHUNKS = ((0, 2), (2, 2))
VMEM_LIMIT = 56 * 1024 * 1024


def lane_iota(rows):
    return lax.broadcasted_iota(jnp.int32, (rows, LANES), 1)


def pack_kernel(slots, first, pattern_ref, jac_ref, out_ref):
    box = pl.program_id(0)
    low_half = lane_iota(1) < BL
    for slot in range(slots):
        base = (box * 4 + first + slot) * (NB * NB)

        def row_mask(p, half):
            low = pattern_ref[base + p * NB + 2 * half].astype(jnp.float32)
            high = pattern_ref[base + p * NB + 2 * half + 1].astype(jnp.float32)
            return jnp.where(low_half, low, high)

        right = []
        for p in range(NB):
            rows = min(SR, (p + 1) * BL) - p * BL
            span = pl.ds(p * BL, rows)
            left = jac_ref[0, slot, span, 0:LANES].astype(jnp.float32) * row_mask(p, 0)
            part = jac_ref[0, slot, span, LANES:SP].astype(jnp.float32) * row_mask(p, 1)
            if p == NB - 1:
                inside = lax.broadcasted_iota(jnp.int32, (rows, LANES), 0) < S - p * BL
                left = jnp.where(inside, left, 0.0)
                part = jnp.where(inside, part, 0.0)
            out_ref[0, slot, span, :] = left.astype(jnp.bfloat16)
            right.append(part)
        right = jnp.concatenate(right, axis=0)
        half_rows = SR // 2
        lanes = lane_iota(half_rows)
        middle = jnp.where(
            lanes < BL, right[:half_rows], pltpu.roll(right[half_rows:], BL, 1)
        )
        out_ref[0, slot, pl.ds(SR, half_rows), :] = middle.astype(jnp.bfloat16)
        lanes = lane_iota(BL)
        last = jnp.concatenate([right[192:SR], jnp.zeros((32, LANES), jnp.float32)], axis=0)
        edge = jnp.where(
            lanes < 32,
            pltpu.roll(right[0:64], 64, 1),
            jnp.where(
                lanes < 64,
                pltpu.roll(right[64:128], 96, 1),
                jnp.where(lanes < 96, right[128:192], pltpu.roll(last, 32, 1)),
            ),
        )
        out_ref[0, slot, pl.ds(SR + half_rows, BL), :] = edge.astype(jnp.bfloat16)


def pack_chunk(jacobian, pattern_flat, first, slots):
    boxes = jacobian.shape[0]
    return pl.pallas_call(
        functools.partial(pack_kernel, slots, first),
        grid=(boxes,),
        in_specs=[
            pl.BlockSpec(memory_space=pltpu.SMEM),
            pl.BlockSpec((1, slots, SP, SP), lambda b: (b, first // slots, 0, 0)),
        ],
        out_specs=pl.BlockSpec((1, slots, PACK, LANES), lambda b: (b, 0, 0, 0)),
        out_shape=jax.ShapeDtypeStruct((boxes, slots, PACK, LANES), jnp.bfloat16),
        compiler_params=pltpu.CompilerParams(vmem_limit_bytes=VMEM_LIMIT),
        cost_estimate=pl.CostEstimate(
            flops=0, bytes_accessed=boxes * slots * 230000, transcendentals=0
        ),
        name="pack_chunk",
    )(pattern_flat, jacobian)


def unpack(packed_ref, item, dense_ref, member):
    half_rows = SR // 2
    dense_ref[member, :, 0:LANES] = packed_ref[item, pl.ds(0, SR), :]
    middle = packed_ref[item, pl.ds(SR, half_rows), :].astype(jnp.float32)
    edge = packed_ref[item, pl.ds(SR + half_rows, BL), :].astype(jnp.float32)
    high = pltpu.roll(middle, BL, 1)

    def put(row, rows, low, rest):
        lanes = lane_iota(rows)
        dense_ref[member, pl.ds(row, rows), LANES:SP] = jnp.where(
            lanes < BL, low, rest
        ).astype(jnp.bfloat16)

    put(0, 64, middle[0:64], pltpu.roll(edge, 64, 1))
    shifted = pltpu.roll(edge, 32, 1)
    put(64, 48, middle[64:112], shifted[0:48])
    put(112, 16, high[0:16], shifted[48:64])
    put(128, 64, high[16:80], edge)
    put(192, 32, high[80:112], pltpu.roll(edge[0:32], 96, 1))


def solve_kernel(items, first_call, *refs):
    if first_call:
        plan_ref, packed_hbm, state_hbm, out_hbm, edge_ref = refs[:5]
        scratch = refs[5:]
    else:
        plan_ref, packed_hbm, state_hbm, _, edge_in, out_hbm, edge_ref = refs[:7]
        scratch = refs[7:]
    packed, state, dense, right, left_over, mapped_ref, guess, arrived, state_sem, sent = scratch
    live = plan_ref[3 * items]
    groups = (live + GROUP - 1) // GROUP

    def fetch(place):
        source = plan_ref[place]
        return pltpu.make_async_copy(
            packed_hbm.at[source], packed.at[place], arrived.at[place]
        )

    def start_fetch(place, carry):
        fetch(place).start()
        return carry

    lax.fori_loop(0, groups * GROUP, start_fetch, 0)
    state_copy = pltpu.make_async_copy(state_hbm, state, state_sem)
    state_copy.start()
    right[...] = jnp.zeros_like(right)
    if first_call:
        edge_ref[...] = jnp.zeros_like(edge_ref)
    else:
        edge_ref[...] = edge_in[...]
    state_copy.wait()
    edge_lane = lane_iota(SR) // 4

    def send(buffer, member, tile):
        return pltpu.make_async_copy(
            guess.at[buffer, member], out_hbm.at[tile], sent.at[buffer, member]
        )

    def drain(group_no):
        for member in range(GROUP):
            place = group_no * GROUP + member

            @pl.when(place < live)
            def _():
                send(group_no % 2, member, plan_ref[items + place]).wait()

    def one_group(group_no, carry):
        buffer = group_no % 2
        places = [group_no * GROUP + member for member in range(GROUP)]
        tiles = [plan_ref[items + place] for place in places]
        counts = [plan_ref[2 * items + place] for place in places]

        @pl.when(group_no >= 2)
        def _():
            drain(group_no - 2)

        for member in range(GROUP):
            fetch(places[member]).wait()
        for member in range(GROUP):
            unpack(packed, places[member], dense, member)
        for member in range(GROUP):
            source = jnp.minimum(tiles[member], state.shape[0] - 1)
            start_value = state[source]
            right[member, 0:SR, 0:LANES] = start_value
            guess[buffer, member] = start_value.astype(jnp.float32)
        for member in range(GROUP):
            remainder = jnp.dot(
                dense[member], right[member, :, 0:LANES], preferred_element_type=jnp.float32
            )
            left_over[member] = remainder
            high = remainder.astype(jnp.bfloat16)
            right[member, 0:SR, 0:LANES] = high
            right[member, 0:SR, LANES:SP] = (remainder - high.astype(jnp.float32)).astype(
                jnp.bfloat16
            )

        def advance(turn_no, inner):
            for member in range(GROUP):
                product = jnp.dot(
                    dense[member], right[member], preferred_element_type=jnp.float32
                )
                remainder = left_over[member]
                mapped = remainder - (product[:, 0:LANES] + product[:, LANES:SP])
                mapped_ref[member] = mapped
                above = jnp.sum(remainder * mapped, axis=0, keepdims=True)
                below = jnp.sum(mapped * mapped, axis=0, keepdims=True) + EPSILON
                step = jnp.where(turn_no < counts[member], above / below, 0.0)
                guess[buffer, member] += step * remainder
                remainder = remainder - step * mapped_ref[member]
                left_over[member] = remainder
                high = remainder.astype(jnp.bfloat16)
                right[member, 0:SR, 0:LANES] = high
                right[member, 0:SR, LANES:SP] = (
                    remainder - high.astype(jnp.float32)
                ).astype(jnp.bfloat16)
            return inner

        lax.fori_loop(0, counts[0], advance, 0)
        for member in range(GROUP):
            result = guess[buffer, member]
            tile = tiles[member]
            edge_ref[...] = jnp.where(
                edge_lane == tile, pltpu.roll(result, (4 * tile + 2) % LANES, 1), edge_ref[...]
            )

            @pl.when(places[member] < live)
            def _():
                send(buffer, member, tile).start()
        return carry

    lax.fori_loop(0, groups, one_group, 0)

    for back in range(2):
        @pl.when(groups > back)
        def _():
            drain(groups - 1 - back)


def solve_chunk(plan, packed, state, reacted, edge):
    items = packed.shape[0]
    tiles = state.shape[0]
    first_call = reacted is None
    out_shape = (
        jax.ShapeDtypeStruct((tiles, SR, LANES), jnp.float32),
        jax.ShapeDtypeStruct((SR, LANES), jnp.float32),
    )
    hbm = pl.BlockSpec(memory_space=pl.ANY)
    vmem = pl.BlockSpec(memory_space=pltpu.VMEM)
    in_specs = [pl.BlockSpec(memory_space=pltpu.SMEM), hbm, hbm]
    operands = [plan, packed, state]
    aliases = {}
    if not first_call:
        in_specs += [hbm, vmem]
        operands += [reacted, edge]
        aliases = {3: 0}
    return pl.pallas_call(
        functools.partial(solve_kernel, items, first_call),
        in_specs=in_specs,
        out_specs=(hbm, vmem),
        out_shape=out_shape,
        input_output_aliases=aliases,
        scratch_shapes=[
            pltpu.VMEM((items, PACK, LANES), jnp.bfloat16),
            pltpu.VMEM((tiles, SR, LANES), jnp.bfloat16),
            pltpu.VMEM((GROUP, SR, SP), jnp.bfloat16),
            pltpu.VMEM((GROUP, SP, SP), jnp.bfloat16),
            pltpu.VMEM((GROUP, SR, LANES), jnp.float32),
            pltpu.VMEM((GROUP, SR, LANES), jnp.float32),
            pltpu.VMEM((2, GROUP, SR, LANES), jnp.float32),
            pltpu.SemaphoreType.DMA((items,)),
            pltpu.SemaphoreType.DMA,
            pltpu.SemaphoreType.DMA((2, GROUP)),
        ],
        compiler_params=pltpu.CompilerParams(vmem_limit_bytes=VMEM_LIMIT),
        cost_estimate=pl.CostEstimate(
            flops=items * 300_000_000, bytes_accessed=items * 200000, transcendentals=0
        ),
        name="solve_chunk",
    )(*operands)


def message_kernel(tiles, block_hbm, low_ref, high_ref, down_ref, up_ref, copied):
    copies = [
        pltpu.make_async_copy(block_hbm.at[tiles - 2 : tiles], down_ref.at[0:2], copied.at[0]),
        pltpu.make_async_copy(block_hbm.at[0:2], up_ref.at[0:2], copied.at[1]),
    ]
    for copy in copies:
        copy.start()
    lanes = lane_iota(SR)
    for row, out_ref in ((tiles - 1, down_ref), (0, up_ref)):
        out_ref[2] = jnp.where(
            lanes == 0,
            pltpu.roll(low_ref[...], (-(4 * row + 1)) % LANES, 1),
            pltpu.roll(high_ref[...], (-(4 * row + 3)) % LANES, 1),
        )
    for copy in copies:
        copy.wait()


def make_messages(block, low, high):
    tiles = block.shape[0]
    vmem = pl.BlockSpec(memory_space=pltpu.VMEM)
    shape = jax.ShapeDtypeStruct((3, SR, LANES), jnp.float32)
    return pl.pallas_call(
        functools.partial(message_kernel, tiles),
        in_specs=[pl.BlockSpec(memory_space=pl.ANY), vmem, vmem],
        out_specs=(vmem, vmem),
        out_shape=(shape, shape),
        scratch_shapes=[pltpu.SemaphoreType.DMA((2,))],
        name="make_messages",
    )(block, low, high)


def diffuse_kernel(tiles, inside_ref, block_hbm, above_ref, below_ref, low_ref, high_ref,
                   own_ref, rate_ref, out_ref, rows, copied):
    copy = pltpu.make_async_copy(block_hbm, rows.at[2 : tiles + 2], copied)
    copy.start()
    rows[0:2] = above_ref[0:2]
    rows[tiles + 2 : tiles + 4] = below_ref[0:2]
    lanes = lane_iota(8)
    column = lanes % 4
    has_above, has_below = inside_ref[0], inside_ref[1]
    has_side = jnp.where(column < 2, inside_ref[2], inside_ref[3])
    copy.wait()

    def slab(start, kept):
        span = pl.ds(start, 8)
        rate = rate_ref[span, :]
        own = own_ref[span, :]
        ghost = jnp.where(column < 2, low_ref[span, :], high_ref[span, :])
        corner_above = above_ref[2, span, :]
        corner_below = below_ref[2, span, :]

        up = pltpu.roll(ghost, 4, 1)
        up = jnp.where(lanes == 1, pltpu.roll(corner_above, 1, 1), up)
        up = jnp.where(lanes == 2, pltpu.roll(corner_above, 3, 1), up)
        down = pltpu.roll(ghost, LANES - 4, 1)
        down = jnp.where(lanes == LANES - 3, pltpu.roll(corner_below, LANES - 3, 1), down)
        down = jnp.where(lanes == LANES - 2, pltpu.roll(corner_below, LANES - 1, 1), down)
        side = jnp.where(
            column == 1,
            pltpu.roll(own, LANES - 1, 1) + pltpu.roll(ghost, 1, 1),
            pltpu.roll(own, 1, 1) + pltpu.roll(ghost, LANES - 1, 1),
        )
        later = (ghost + rate * (up + down + side - 4.0 * ghost)) * has_side

        def swapped(edge):
            return jnp.where(column == 2, pltpu.roll(edge, 1, 1), pltpu.roll(edge, LANES - 1, 1))

        edge_now, edge_later = swapped(ghost), swapped(later)

        def step(middle, over, under, edge):
            left = jnp.where(lanes == 0, edge, pltpu.roll(middle, 1, 1))
            right = jnp.where(lanes == LANES - 1, edge, pltpu.roll(middle, LANES - 1, 1))
            return middle + rate * (over + under + left + right - 4.0 * middle)

        def edge_of(edge, row):
            return pltpu.roll(edge, (-(4 * row + 2)) % LANES, 1)

        def first(row):
            if row == -1:
                edge = corner_above
            elif row == tiles:
                edge = corner_below
            else:
                edge = edge_of(edge_now, row)
            value = step(
                rows[row + 2, span, :], rows[row + 1, span, :], rows[row + 3, span, :], edge
            )
            if row == -1:
                return value * has_above
            if row == tiles:
                return value * has_below
            return value

        over, middle = first(-1), first(0)
        for row in range(tiles):
            under = first(row + 1)
            value = step(middle, over, under, edge_of(edge_later, row))
            out_ref[pl.ds(start * tiles + row, kept, stride=tiles), :] = value[0:kept]
            over, middle = middle, under

    def whole_slab(number, carry):
        slab(pl.multiple_of(number * 8, 8), 8)
        return carry

    lax.fori_loop(0, S // 8, whole_slab, 0)
    if S % 8:
        slab(S // 8 * 8, S % 8)


def diffuse(inside, block, above, below, low, high, own, rate):
    tiles = block.shape[0]
    vmem = pl.BlockSpec(memory_space=pltpu.VMEM)
    return pl.pallas_call(
        functools.partial(diffuse_kernel, tiles),
        in_specs=[
            pl.BlockSpec(memory_space=pltpu.SMEM),
            pl.BlockSpec(memory_space=pl.ANY),
        ]
        + [vmem] * 6,
        out_specs=vmem,
        out_shape=jax.ShapeDtypeStruct((S * tiles, LANES), jnp.float32),
        scratch_shapes=[
            pltpu.VMEM((tiles + 4, SR, LANES), jnp.float32),
            pltpu.SemaphoreType.DMA,
        ],
        compiler_params=pltpu.CompilerParams(vmem_limit_bytes=VMEM_LIMIT),
        name="diffuse",
    )(inside, block, above, below, low, high, own, rate)


def make_plan(slot_tile, counts):
    items = slot_tile.shape[0]
    tiles = counts.shape[0]
    live = slot_tile >= 0
    turns = jnp.where(live, counts[jnp.where(live, slot_tile, 0)], 0)
    _, source, tile, turns = lax.sort(
        (
            jnp.where(live, -turns, 1),
            jnp.arange(items, dtype=jnp.int32),
            jnp.where(live, slot_tile, tiles),
            turns,
        ),
        num_keys=1,
    )
    return jnp.concatenate([source, tile, turns, jnp.sum(live, dtype=jnp.int32)[None]])


def shifted(value, axis, by):
    count = lax.axis_size(axis)
    pairs = [(i, i + by) for i in range(count) if 0 <= i + by < count]
    return lax.ppermute(value, axis, pairs)


def on_device(species_state, stiffness, send_list, jacobian, pattern, diffusivity):
    boxes = lax.axis_size("box")
    tiles = species_state.shape[0]
    slots = jacobian.shape[0] // boxes
    by_box = jacobian.reshape(boxes, slots, SP, SP)
    pattern_flat = pattern.reshape(-1)
    received = []
    for first, count in CHUNKS:
        packed = pack_chunk(by_box, pattern_flat, first, count)
        arrived = lax.all_to_all(packed, "box", split_axis=0, concat_axis=0, tiled=True)
        received.append(arrived.reshape(boxes * count, PACK, LANES))

    counts = stiffness[:, 0]
    table = send_list.reshape(boxes, slots)
    plans = [
        make_plan(table[:, first : first + count].reshape(-1), counts) for first, count in CHUNKS
    ]
    state = jnp.pad(species_state, ((0, 0), (0, SR - S), (0, 0)))
    reacted = edge = None
    for plan, packed in zip(plans, received):
        reacted, edge = solve_chunk(plan, packed, state, reacted, edge)

    low = shifted(edge, "bal", 1)
    high = shifted(edge, "bal", -1)
    down, up = make_messages(reacted, low, high)
    above = shifted(down, "box", 1)
    below = shifted(up, "box", -1)
    place = lax.axis_index("box"), lax.axis_index("bal")
    inside = jnp.stack(
        [
            place[0] > 0,
            place[0] < boxes - 1,
            place[1] > 0,
            place[1] < lax.axis_size("bal") - 1,
        ]
    ).astype(jnp.float32)
    rate = jnp.broadcast_to(jnp.pad(diffusivity, (0, SR - S))[:, None], (SR, LANES))
    field = diffuse(inside, reacted, above, below, low, high, edge, rate)
    return field.reshape(S, tiles, LANES).transpose(1, 0, 2)


def solution(mesh):
    in_specs = (
        P("box", None, "bal"),
        P("box", "bal"),
        P("box", "bal", None, None),
        P("box", "bal", None, None),
        P("box", "bal", None, None),
        P(),
    )
    return jax.shard_map(
        on_device,
        mesh=mesh,
        in_specs=in_specs,
        out_specs=P("box", None, "bal"),
        check_vma=False,
    )
```

```python
import functools

import jax
import numpy as np
import jax.numpy as jnp
from jax import lax
from jax.experimental import pallas as pl
from jax.experimental.pallas import tpu as pltpu
from jax.sharding import PartitionSpec as P

S = 218
SR = 224
SP = 256
BL = 64
NB = 4
PACK = 400
LANES = 128
EPSILON = 1e-06
GROUP = 8
SLOTS = 4
CHUNKS = ((0, 3), (3, 1))
PACK_BOXES = 4
SPECIES = 56
WIDE_VMEM = 61 * 1024 * 1024


def lane_iota(rows):
    return lax.broadcasted_iota(jnp.int32, (rows, LANES), 1)


def make_plan(table, counts):
    slots, boxes = table.shape
    tiles = counts.shape[1]
    size = float(LANES)
    filler = jnp.full((slots, LANES - boxes), -1.0, jnp.float32)
    spread = jnp.concatenate([table.astype(jnp.float32), filler], axis=1)
    counts = jnp.concatenate(
        [counts.astype(jnp.float32), jnp.zeros((1, LANES - tiles), jnp.float32)], axis=1
    )
    lane = lane_iota(LANES).astype(jnp.float32)
    item = lax.broadcasted_iota(jnp.int32, (LANES, LANES), 0).astype(jnp.float32)
    row = jnp.full((1, LANES), -1.0, jnp.float32)
    for slot in range(slots):
        part = pltpu.roll(spread, slot * boxes, 1)[slot : slot + 1] if slot else spread[0:1]
        here = (lane_iota(1) >= slot * boxes) & (lane_iota(1) < (slot + 1) * boxes)
        row = jnp.where(here, part, row)
    tile = jnp.transpose(jnp.broadcast_to(row, (LANES, LANES)))
    turns = jnp.sum(jnp.where(tile == lane, counts, 0.0), axis=1, keepdims=True)
    turns = jnp.broadcast_to(turns, (LANES, LANES))
    live = tile >= 0.0
    early_size = CHUNKS[0][1] * boxes
    early = live & (item < early_size)
    weight = (size - turns) * size + item

    def rank(key):
        smaller = jnp.where(jnp.transpose(key) < key, 1.0, 0.0)
        return jnp.broadcast_to(jnp.sum(smaller, axis=1, keepdims=True), (LANES, LANES))

    late = 4.0 * size * size
    begun = jnp.sum(jnp.where(early, 1.0, 0.0), axis=0, keepdims=True)
    begun = jnp.floor(begun * (1.0 / GROUP)) * GROUP
    chosen = early & (rank(jnp.where(early, weight, late + item)) < begun)
    place = rank(weight + jnp.where(chosen, 0.0, jnp.where(live, late, 2.0 * late)))
    slot_of = jnp.floor(item * (1.0 / boxes))
    box_of = item - slot_of * boxes
    width = float(CHUNKS[0][1])
    source = jnp.where(item < early_size, box_of * width + slot_of, item)
    rows = [
        jnp.sum(jnp.where(place == lane, value, 0.0), axis=0, keepdims=True)
        for value in (source, tile, turns)
    ]
    rows += [begun, jnp.zeros((4, LANES), jnp.float32)]
    return jnp.concatenate(rows, axis=0).astype(jnp.int32)


def pack_kernel(pattern_ref, table_ref, counts_ref, jac_ref, plan_ref, *out_refs):
    @pl.when(pl.program_id(0) == 0)
    def _():
        plan_ref[...] = make_plan(table_ref[...], counts_ref[...])

    low_half = lane_iota(1) < BL
    half_rows = SR // 2
    tail = SR - (NB - 1) * BL
    inside = lax.broadcasted_iota(jnp.int32, (tail, LANES), 0) < S - (NB - 1) * BL
    inside = inside.astype(jnp.float32).astype(jnp.bfloat16)
    middle_lane = lane_iota(half_rows)
    edge_lane = lane_iota(BL)

    def one_box(inner, carry):
        box = pl.program_id(0) * PACK_BOXES + inner
        for slot in range(SLOTS):
            chunk = next(k for k, (at, n) in enumerate(CHUNKS) if at <= slot < at + n)
            put = functools.partial(out_refs[chunk].__setitem__)
            place = slot - CHUNKS[chunk][0]
            held = box * SLOTS + slot
            right = []
            for p in range(NB):
                rows = min(SR, (p + 1) * BL) - p * BL
                parts = []
                for half in range(2):
                    mask = jnp.where(
                        low_half,
                        pattern_ref[p, 2 * half, held].astype(jnp.float32),
                        pattern_ref[p, 2 * half + 1, held].astype(jnp.float32),
                    ).astype(jnp.bfloat16)
                    value = (
                        jac_ref[inner, slot, p * BL : p * BL + rows, half * LANES : (half + 1) * LANES]
                        * mask
                    )
                    parts.append(value * inside if p == NB - 1 else value)
                put((inner, place, slice(p * BL, p * BL + rows), slice(None)), parts[0])
                right.append(parts[1])
            upper = jnp.concatenate([right[0], right[1][: half_rows - BL]], axis=0)
            lower = jnp.concatenate([right[1][half_rows - BL :], right[2], right[3]], axis=0)
            middle = jnp.where(middle_lane < BL, upper, pltpu.roll(lower, BL, 1))
            put((inner, place, slice(SR, SR + half_rows), slice(None)), middle)
            last = jnp.concatenate([right[3], jnp.zeros((BL - tail, LANES), jnp.bfloat16)], axis=0)
            edge = jnp.where(
                edge_lane < 64,
                jnp.where(edge_lane < 32, pltpu.roll(right[0], 64, 1), pltpu.roll(right[1], 96, 1)),
                jnp.where(edge_lane < 96, right[2], pltpu.roll(last, 32, 1)),
            )
            put((inner, place, slice(SR + half_rows, PACK), slice(None)), edge)
        return carry

    lax.fori_loop(0, PACK_BOXES, one_box, 0)


def pack_all(jacobian, pattern, table, counts):
    boxes = jacobian.shape[0]
    return pl.pallas_call(
        pack_kernel,
        grid=(boxes // PACK_BOXES,),
        in_specs=[
            pl.BlockSpec(memory_space=pltpu.SMEM),
            pl.BlockSpec(table.shape, lambda b: (0, 0)),
            pl.BlockSpec(counts.shape, lambda b: (0, 0)),
            pl.BlockSpec((PACK_BOXES, SLOTS, SR, SP), lambda b: (b, 0, 0, 0)),
        ],
        out_specs=[pl.BlockSpec((8, LANES), lambda b: (0, 0))]
        + [
            pl.BlockSpec((PACK_BOXES, n, PACK, LANES), lambda b: (b, 0, 0, 0)) for _, n in CHUNKS
        ],
        out_shape=[jax.ShapeDtypeStruct((8, LANES), jnp.int32)]
        + [
            jax.ShapeDtypeStruct((boxes, n, PACK, LANES), jnp.bfloat16) for _, n in CHUNKS
        ],
        compiler_params=pltpu.CompilerParams(vmem_limit_bytes=WIDE_VMEM),
        name="pack_all",
    )(pattern, table, counts, jacobian)


def unpack(packed_ref, item, dense_ref):
    half_rows = SR // 2
    dense_ref[:, 0:LANES] = packed_ref[item, pl.ds(0, SR), :]
    middle = packed_ref[item, pl.ds(SR, half_rows), :]
    edge = packed_ref[item, pl.ds(SR + half_rows, BL), :]
    high = pltpu.roll(middle, BL, 1)

    def put(row, rows, low, rest):
        dense_ref[pl.ds(row, rows), LANES:SP] = jnp.where(lane_iota(rows) < BL, low, rest)

    put(0, 64, middle[0:64], pltpu.roll(edge, 64, 1))
    shifted = pltpu.roll(edge, 32, 1)
    put(64, 48, middle[64:112], shifted[0:48])
    put(112, 16, high[0:16], shifted[48:64])
    put(128, 64, high[16:80], edge)
    put(192, 32, high[80:112], pltpu.roll(edge[0:32], 96, 1))


def solve_kernel(chunk, *refs):
    if chunk == 0:
        plan_ref, state_hbm, packed_hbm, out_hbm, edge_ref = refs[:5]
        scratch = refs[5:]
    else:
        plan_ref, state_hbm, packed_hbm, second_hbm, _, edge_in, out_hbm, edge_ref = refs[:8]
        scratch = refs[8:]
    packed, state, outgoing, arrived, state_sem, sent = scratch[:6]
    dense, right, left_over, mapped, guess, sums = (
        scratch[6 + GROUP * kind : 6 + GROUP * (kind + 1)] for kind in range(6)
    )
    tiles = state.shape[0]
    begun = plan_ref[3, 0]
    base = 0 if chunk == 0 else begun
    groups = (begun if chunk == 0 else tiles - begun) // GROUP
    state_copy = pltpu.make_async_copy(state_hbm, state, state_sem)
    state_copy.start()

    def fetch(place, origin, at):
        return pltpu.make_async_copy(origin.at[at], packed.at[place], arrived.at[place])

    def start_fetch(place, carry):
        at = plan_ref[0, base + place]
        if chunk == 0:
            fetch(place, packed_hbm, at).start()
        else:
            early = packed_hbm.shape[0]

            @pl.when(at < early)
            def _():
                fetch(place, packed_hbm, at).start()

            @pl.when(at >= early)
            def _():
                fetch(place, second_hbm, at - early).start()

        return carry

    lax.fori_loop(0, groups * GROUP, start_fetch, 0)
    for member in range(GROUP):
        right[member][...] = jnp.zeros_like(right[member])
    if chunk == 0:
        edge_ref[...] = jnp.zeros_like(edge_ref)
    else:
        edge_ref[...] = edge_in[...]
    state_copy.wait()
    edge_lane = lane_iota(SR) // 4

    def send(buffer, member, tile):
        return pltpu.make_async_copy(
            outgoing.at[buffer, member], out_hbm.at[tile], sent.at[buffer, member]
        )

    def drain(group_no):
        for member in range(GROUP):
            send(group_no % 2, member, plan_ref[1, base + group_no * GROUP + member]).wait()

    def split(member, row, rows, remainder):
        high = remainder.astype(jnp.bfloat16)
        span = slice(row, row + rows)
        right[member][span, 0:LANES] = high
        right[member][span, LANES:SP] = (remainder - high.astype(jnp.float32)).astype(
            jnp.bfloat16
        )

    def multiply(member):
        return jnp.dot(
            dense[member][...], right[member][...], preferred_element_type=jnp.float32
        )

    def measure(member, product):
        above = jnp.zeros((8, LANES), jnp.float32)
        below = jnp.zeros((8, LANES), jnp.float32)
        for row in range(0, SR, 8):
            span = slice(row, row + 8)
            remainder = left_over[member][span, :]
            value = remainder - (product[span, 0:LANES] + product[span, LANES:SP])
            mapped[member][span, :] = value
            above = above + remainder * value
            below = below + value * value
        return above, below

    def move(member, above, below, active):
        above = jnp.sum(above, axis=0, keepdims=True)
        below = jnp.sum(below, axis=0, keepdims=True) + EPSILON
        step = jnp.where(active, above / below, 0.0)
        for row in range(0, SR, 16):
            span = slice(row, row + 16)
            remainder = left_over[member][span, :]
            guess[member][span, :] += step * remainder
            remainder = remainder - step * mapped[member][span, :]
            left_over[member][span, :] = remainder
            split(member, row, 16, remainder)

    def keep_sums(member, above, below):
        sums[member][0:8, :] = above
        sums[member][8:16, :] = below

    def one_group(group_no, carry):
        buffer = group_no % 2
        places = [group_no * GROUP + member for member in range(GROUP)]
        chosen = [plan_ref[1, base + place] for place in places]
        counts = [plan_ref[2, base + place] for place in places]

        for member in range(GROUP):
            fetch(places[member], packed_hbm, 0).wait()
        for member in range(GROUP):
            unpack(packed, places[member], dense[member])
            start_value = state[chosen[member]]
            right[member][0:SR, 0:LANES] = start_value
            guess[member][...] = start_value.astype(jnp.float32)
        for member in range(GROUP):
            remainder = jnp.dot(
                dense[member][...],
                right[member][:, 0:LANES],
                preferred_element_type=jnp.float32,
            )
            left_over[member][...] = remainder
            split(member, 0, SR, remainder)

        half = GROUP // 2
        for member in range(half, GROUP):
            keep_sums(member, *measure(member, multiply(member)))

        def advance(turn_no, inner):
            for one, other in zip(range(half), range(half, GROUP)):
                product = multiply(one)
                move(other, sums[other][0:8, :], sums[other][8:16, :], turn_no < counts[other])
                next_product = multiply(other)
                move(one, *measure(one, product), turn_no < counts[one])
                keep_sums(other, *measure(other, next_product))
            return inner

        lax.fori_loop(0, functools.reduce(jnp.maximum, counts), advance, 0)

        @pl.when(group_no >= 2)
        def _():
            drain(group_no - 2)

        for member in range(GROUP):
            result = guess[member][...]
            outgoing[buffer, member] = result
            tile = chosen[member]
            edge_ref[...] = jnp.where(
                edge_lane == tile, pltpu.roll(result, (4 * tile + 2) % LANES, 1), edge_ref[...]
            )
            send(buffer, member, tile).start()
        return carry

    lax.fori_loop(0, groups, one_group, 0)

    for back in range(2):
        @pl.when(groups > back)
        def _():
            drain(groups - 1 - back)


def solve_chunk(chunk, plan, state, packed, reacted, edge):
    tiles = state.shape[0]
    out_shape = (
        jax.ShapeDtypeStruct((tiles, SR, LANES), jnp.float32),
        jax.ShapeDtypeStruct((SR, LANES), jnp.float32),
    )
    anywhere = pl.BlockSpec(memory_space=pl.ANY)
    vmem = pl.BlockSpec(memory_space=pltpu.VMEM)
    in_specs = [pl.BlockSpec(memory_space=pltpu.SMEM), anywhere]
    in_specs += [anywhere] * (chunk + 1)
    operands = [plan, state, *packed[: chunk + 1]]
    aliases = {}
    if chunk:
        in_specs += [anywhere, vmem]
        operands += [reacted, edge]
        aliases = {4: 0}
    tile_values = pltpu.VMEM((SR, LANES), jnp.float32)
    return pl.pallas_call(
        functools.partial(solve_kernel, chunk),
        in_specs=in_specs,
        out_specs=(anywhere, vmem),
        out_shape=out_shape,
        input_output_aliases=aliases,
        scratch_shapes=[
            pltpu.VMEM((tiles, PACK, LANES), jnp.bfloat16),
            pltpu.VMEM((tiles, SR, LANES), jnp.bfloat16),
            pltpu.VMEM((2, GROUP, SR, LANES), jnp.float32),
            pltpu.SemaphoreType.DMA((tiles,)),
            pltpu.SemaphoreType.DMA,
            pltpu.SemaphoreType.DMA((2, GROUP)),
        ]
        + [pltpu.VMEM((SR, SP), jnp.bfloat16)] * GROUP
        + [pltpu.VMEM((SP, SP), jnp.bfloat16)] * GROUP
        + [tile_values] * (3 * GROUP)
        + [pltpu.VMEM((16, LANES), jnp.float32)] * GROUP,
        compiler_params=pltpu.CompilerParams(vmem_limit_bytes=WIDE_VMEM),
        cost_estimate=pl.CostEstimate(
            flops=16 * 300_000_000, bytes_accessed=16 * 200000, transcendentals=0
        ),
        name="solve_chunk",
    )(*operands)


def message_kernel(bottom_ref, top_ref, low_ref, high_ref, down_ref, up_ref):
    tiles = LANES // 4
    down_ref[0:2] = bottom_ref[...].astype(jnp.bfloat16)
    up_ref[0:2] = top_ref[...].astype(jnp.bfloat16)
    lanes = lane_iota(SR)
    for row, out_ref in ((tiles - 1, down_ref), (0, up_ref)):
        out_ref[2] = jnp.where(
            lanes == 0,
            pltpu.roll(low_ref[...], (-(4 * row + 1)) % LANES, 1),
            pltpu.roll(high_ref[...], (-(4 * row + 3)) % LANES, 1),
        ).astype(jnp.bfloat16)


def make_messages(block, low, high):
    tiles = block.shape[0]
    shape = jax.ShapeDtypeStruct((3, SR, LANES), jnp.bfloat16)
    edge = pl.BlockSpec((SR, LANES), lambda i: (0, 0))
    message = pl.BlockSpec((3, SR, LANES), lambda i: (0, 0, 0))
    return pl.pallas_call(
        message_kernel,
        grid=(1,),
        in_specs=[
            pl.BlockSpec((2, SR, LANES), lambda i: (tiles // 2 - 1, 0, 0)),
            pl.BlockSpec((2, SR, LANES), lambda i: (0, 0, 0)),
            edge,
            edge,
        ],
        out_specs=(message, message),
        out_shape=(shape, shape),
        compiler_params=pltpu.CompilerParams(vmem_limit_bytes=WIDE_VMEM),
        name="make_messages",
    )(block, block, low, high)


def beside(value, lanes):
    return jnp.where(lanes == 0, 0.0, pltpu.roll(value, 1, 1)) + jnp.where(
        lanes == LANES - 1, 0.0, pltpu.roll(value, LANES - 1, 1)
    )


def inner_kernel(tiles, block_ref, rate_ref, both_ref, out_ref):
    zero = jnp.zeros((1, 8, LANES), jnp.float32)

    def around(value, by):
        gap = jnp.concatenate([zero] * by, axis=0)
        return jnp.concatenate([gap, value[: tiles - by]], axis=0) + jnp.concatenate(
            [value[by:], gap], axis=0
        )

    for number in range(SPECIES // 8):
        span = slice(number * 8, number * 8 + 8)
        rate = rate_ref[span, :]
        keep = 1.0 - 4.0 * rate
        square = rate * rate
        cells = block_ref[:, span, :]
        flat = cells.reshape(tiles * 8, LANES)
        high = flat.astype(jnp.bfloat16)
        low = (flat - high.astype(jnp.float32)).astype(jnp.bfloat16)
        product = jnp.dot(
            jnp.concatenate([high, low], axis=1), both_ref[...], preferred_element_type=jnp.float32
        )
        once = product[:, 0:LANES].reshape(tiles, 8, LANES)
        twice = product[:, LANES:].reshape(tiles, 8, LANES)
        near = (2.0 * keep * rate) * (around(cells, 1) + once)
        sides = around(once, 1)
        far = square * ((around(cells, 2) + twice) + (sides + sides))
        own = keep * keep + 2.0 * square
        end = keep * keep + square
        value = near + far
        out_ref[1 : tiles - 1, span, :] = value[1 : tiles - 1] + own * cells[1 : tiles - 1]
        out_ref[0, span, :] = value[0] + end * cells[0]
        out_ref[tiles - 1, span, :] = value[tiles - 1] + end * cells[tiles - 1]


def diffuse_inside(block, rate):
    tiles = block.shape[0]
    cells = pl.BlockSpec((tiles, SPECIES, LANES), lambda g: (0, g, 0))
    place = np.arange(LANES)
    next_to = (np.abs(place[:, None] - place[None, :]) == 1).astype(np.float32)
    both = np.concatenate([next_to, next_to @ next_to], axis=1)
    both = jnp.asarray(np.concatenate([both, both], axis=0), jnp.bfloat16)
    return pl.pallas_call(
        functools.partial(inner_kernel, tiles),
        grid=(SR // SPECIES,),
        in_specs=[
            cells,
            pl.BlockSpec((SPECIES, LANES), lambda g: (g, 0)),
            pl.BlockSpec((2 * LANES, 2 * LANES), lambda g: (0, 0)),
        ],
        out_specs=cells,
        out_shape=jax.ShapeDtypeStruct(block.shape, jnp.float32),
        compiler_params=pltpu.CompilerParams(vmem_limit_bytes=WIDE_VMEM),
        cost_estimate=pl.CostEstimate(
            flops=tiles * SR * LANES * 20, bytes_accessed=8 * block.size, transcendentals=0
        ),
        name="diffuse_inside",
    )(block, rate, both)


def border_kernel(tiles, inside_ref, inner_ref, top_ref, bottom_ref, above_ref, below_ref,
                  low_ref, high_ref, own_ref, rate_ref, out_ref):
    lanes = lane_iota(8)
    column = lanes % 4
    has_above, has_below = inside_ref[0], inside_ref[1]
    has_side = jnp.where(column < 2, inside_ref[2], inside_ref[3])
    near_edge = (lanes < 2) | (lanes >= LANES - 2)

    def slab(number):
        span = slice(number * 8, number * 8 + 8)
        overall = pl.program_id(0) * (SPECIES // 8) + number
        wide = pl.ds(pl.multiple_of(overall // 2 * 16, 16), 16)

        def read(ref, row):
            both = ref[row, wide, :].astype(jnp.float32)
            return jnp.where(overall % 2 == 0, both[0:8], both[8:16])

        rate = rate_ref[span, :]
        keep = 1.0 - 4.0 * rate
        own = own_ref[span, :]
        ghost = jnp.where(column < 2, low_ref[span, :], high_ref[span, :])

        def rows_beside(near, far, inner, corner, exists):
            left = jnp.where(lanes == 0, corner, pltpu.roll(near, 1, 1))
            right = jnp.where(lanes == LANES - 1, corner, pltpu.roll(near, LANES - 1, 1))
            later = (keep * near + rate * ((far + inner) + (left + right))) * exists
            first = rate * near
            outer = keep * first + rate * (beside(first, lanes) + later)
            return outer, rate * first

        corner_above, corner_below = read(above_ref, 2), read(below_ref, 2)
        row_terms = {}
        row_terms[0], row_terms[1] = rows_beside(
            read(above_ref, 1), read(above_ref, 0), top_ref[0, span, :], corner_above, has_above
        )
        row_terms[tiles - 1], row_terms[tiles - 2] = rows_beside(
            read(below_ref, 0), read(below_ref, 1), bottom_ref[0, span, :], corner_below, has_below
        )

        up = pltpu.roll(ghost, 4, 1)
        up = jnp.where(lanes == 1, pltpu.roll(corner_above, 1, 1), up)
        up = jnp.where(lanes == 2, pltpu.roll(corner_above, 3, 1), up)
        down = pltpu.roll(ghost, LANES - 4, 1)
        down = jnp.where(lanes == LANES - 3, pltpu.roll(corner_below, LANES - 3, 1), down)
        down = jnp.where(lanes == LANES - 2, pltpu.roll(corner_below, LANES - 1, 1), down)
        side = jnp.where(
            column == 1,
            pltpu.roll(own, LANES - 1, 1) + pltpu.roll(ghost, 1, 1),
            pltpu.roll(own, 1, 1) + pltpu.roll(ghost, LANES - 1, 1),
        )
        later = (keep * ghost + rate * ((up + down) + side)) * has_side
        first = rate * ghost
        first_up = jnp.where(lanes < 4, 0.0, pltpu.roll(first, 4, 1))
        first_down = jnp.where(lanes >= LANES - 4, 0.0, pltpu.roll(first, LANES - 4, 1))
        outer = keep * first + rate * ((first_up + first_down) + later)
        second = rate * first
        terms = jnp.where(
            column < 2,
            jnp.where(column == 0, pltpu.roll(second, LANES - 2, 1), pltpu.roll(outer, LANES - 1, 1)),
            jnp.where(column == 2, pltpu.roll(outer, 1, 1), pltpu.roll(second, 2, 1)),
        )
        values = []
        for row in range(tiles):
            value = inner_ref[row, span, :] + jnp.where(
                near_edge, pltpu.roll(terms, (-(4 * row + 2)) % LANES, 1), 0.0
            )
            if row in row_terms:
                value = value + row_terms[row]
            values.append(value)
        out_ref[span, :, :] = jnp.swapaxes(jnp.stack(values, axis=0), 0, 1)

    for number in range(SPECIES // 8):
        slab(number)


def add_borders(inside, inner, block, above, below, low, high, own, rate):
    tiles = block.shape[0]
    message = pl.BlockSpec((3, SR, LANES), lambda g: (0, 0, 0))
    edge = pl.BlockSpec((SPECIES, LANES), lambda g: (g, 0))
    return pl.pallas_call(
        functools.partial(border_kernel, tiles),
        grid=(SR // SPECIES,),
        in_specs=[
            pl.BlockSpec(memory_space=pltpu.SMEM),
            pl.BlockSpec((tiles, SPECIES, LANES), lambda g: (0, g, 0)),
            pl.BlockSpec((1, SPECIES, LANES), lambda g: (0, g, 0)),
            pl.BlockSpec((1, SPECIES, LANES), lambda g: (tiles - 1, g, 0)),
            message,
            message,
            edge,
            edge,
            edge,
            edge,
        ],
        out_specs=pl.BlockSpec((SPECIES, tiles, LANES), lambda g: (g, 0, 0)),
        out_shape=jax.ShapeDtypeStruct((S, tiles, LANES), jnp.float32),
        compiler_params=pltpu.CompilerParams(vmem_limit_bytes=WIDE_VMEM),
        name="add_borders",
    )(inside, inner, block, block, above, below, low, high, own, rate)


def shifted(value, axis, by):
    count = lax.axis_size(axis)
    pairs = [(i, i + by) for i in range(count) if 0 <= i + by < count]
    return lax.ppermute(value, axis, pairs)


def on_device(species_state, stiffness, send_list, jacobian, pattern, diffusivity):
    boxes = lax.axis_size("box")
    tiles = species_state.shape[0]
    slots = jacobian.shape[0] // boxes
    by_box = jacobian.reshape(boxes, slots, SP, SP)
    counts = stiffness.reshape(1, tiles)
    table = send_list.transpose(0, 1, 3, 2).reshape(slots, boxes)
    place = lax.axis_index("box"), lax.axis_index("bal")
    inside = jnp.stack(
        [
            place[0] > 0,
            place[0] < boxes - 1,
            place[1] > 0,
            place[1] < lax.axis_size("bal") - 1,
        ]
    ).astype(jnp.float32)
    rate = jnp.broadcast_to(jnp.pad(diffusivity, (0, SR - S))[:, None], (SR, LANES))
    state = jnp.pad(species_state, ((0, 0), (0, SR - S), (0, 0)))
    by_block = pattern.transpose(1, 2, 3, 0).reshape(NB, NB, boxes * slots)
    plan, first, second = pack_all(by_box, by_block, table, counts)
    first, second, plan, inside, rate, state = lax.optimization_barrier(
        (first, second, plan, inside, rate, state)
    )

    def exchange(packed):
        arrived = lax.all_to_all(packed, "box", split_axis=0, concat_axis=0, tiled=True)
        return arrived.reshape(-1, PACK, LANES)

    first = exchange(first)
    first, second, plan, inside, rate, state = lax.optimization_barrier(
        (first, second, plan, inside, rate, state)
    )
    second = exchange(second)
    reacted, edge = solve_chunk(0, plan, state, (first, second), None, None)
    reacted, edge = solve_chunk(1, plan, state, (first, second), reacted, edge)

    low = shifted(edge, "bal", 1)
    high = shifted(edge, "bal", -1)
    down, up = make_messages(reacted, low, high)
    above = shifted(down, "box", 1)
    below = shifted(up, "box", -1)
    inner = diffuse_inside(reacted, rate)
    field = add_borders(inside, inner, reacted, above, below, low, high, edge, rate)
    return field.transpose(1, 0, 2)


def solution(mesh):
    in_specs = (
        P("box", None, "bal"),
        P("box", "bal"),
        P("box", "bal", None, None),
        P("box", "bal", None, None),
        P("box", "bal", None, None),
        P(),
    )
    return jax.shard_map(
        on_device,
        mesh=mesh,
        in_specs=in_specs,
        out_specs=P("box", None, "bal"),
        check_vma=False,
    )
```

```python
import functools

import jax
import numpy as np
import jax.numpy as jnp
from jax import lax
from jax.experimental import pallas as pl
from jax.experimental.pallas import tpu as pltpu
from jax.sharding import PartitionSpec as P

S = 218
SR = 224
SP = 256
BL = 64
NB = 4
PACK = 400
LANES = 128
EPSILON = 1e-06
GROUP = 8
SLOTS = 4
CHUNKS = ((0, 3), (3, 1))
PACK_BOXES = 8
TURN_SPECIES = 112
SPECIES = 56
WIDE_VMEM = 61 * 1024 * 1024
INNER_VMEM = 48 * 1024 * 1024
TIGHT_VMEM = 40 * 1024 * 1024


def lane_iota(rows):
    return lax.broadcasted_iota(jnp.int32, (rows, LANES), 1)


def make_plan(table, counts):
    slots, boxes = table.shape
    tiles = counts.shape[1]
    size = float(LANES)
    filler = jnp.full((slots, LANES - boxes), -1.0, jnp.float32)
    spread = jnp.concatenate([table.astype(jnp.float32), filler], axis=1)
    counts = jnp.concatenate(
        [counts.astype(jnp.float32), jnp.zeros((1, LANES - tiles), jnp.float32)], axis=1
    )
    lane = lane_iota(LANES).astype(jnp.float32)
    item = lax.broadcasted_iota(jnp.int32, (LANES, LANES), 0).astype(jnp.float32)
    row = jnp.full((1, LANES), -1.0, jnp.float32)
    for slot in range(slots):
        part = pltpu.roll(spread, slot * boxes, 1)[slot : slot + 1] if slot else spread[0:1]
        here = (lane_iota(1) >= slot * boxes) & (lane_iota(1) < (slot + 1) * boxes)
        row = jnp.where(here, part, row)
    tile = jnp.transpose(jnp.broadcast_to(row, (LANES, LANES)))
    turns = jnp.sum(jnp.where(tile == lane, counts, 0.0), axis=1, keepdims=True)
    turns = jnp.broadcast_to(turns, (LANES, LANES))
    live = tile >= 0.0
    early_size = CHUNKS[0][1] * boxes
    early = live & (item < early_size)
    weight = (size - turns) * size + item

    def rank(key):
        smaller = jnp.where(jnp.transpose(key) < key, 1.0, 0.0)
        return jnp.broadcast_to(jnp.sum(smaller, axis=1, keepdims=True), (LANES, LANES))

    late = 4.0 * size * size
    begun = jnp.sum(jnp.where(early, 1.0, 0.0), axis=0, keepdims=True)
    begun = jnp.floor(begun * (1.0 / GROUP)) * GROUP
    chosen = early & (rank(jnp.where(early, weight, late + item)) < begun)
    place = rank(weight + jnp.where(chosen, 0.0, jnp.where(live, late, 2.0 * late)))
    slot_of = jnp.floor(item * (1.0 / boxes))
    box_of = item - slot_of * boxes
    width = float(CHUNKS[0][1])
    source = jnp.where(item < early_size, box_of * width + slot_of, item)
    rows = [
        jnp.sum(jnp.where(place == lane, value, 0.0), axis=0, keepdims=True)
        for value in (source, tile, turns)
    ]
    rows += [begun, jnp.zeros((4, LANES), jnp.float32)]
    return jnp.concatenate(rows, axis=0).astype(jnp.int32)


def pack_kernel(pattern_ref, table_ref, counts_ref, diffusivity_ref, cells_ref, jac_ref,
                plan_ref, rate_ref, state_ref, *out_refs):
    @pl.when(pl.program_id(0) == 0)
    def _():
        plan_ref[...] = make_plan(table_ref[...], counts_ref[...])
        row = jnp.concatenate(
            [diffusivity_ref[...], jnp.zeros((1, SP - S), jnp.float32)], axis=1
        )
        for start in (0, LANES):
            rows = min(LANES, SR - start)
            part = jnp.broadcast_to(row[:, start : start + LANES], (LANES, LANES))
            rate_ref[start : start + rows, :] = jnp.transpose(part)[0:rows]

    state_ref[...] = cells_ref[...].astype(jnp.float32)

    low_half = lane_iota(1) < BL
    half_rows = SR // 2
    tail = SR - (NB - 1) * BL
    inside = lax.broadcasted_iota(jnp.int32, (tail, LANES), 0) < S - (NB - 1) * BL
    inside = inside.astype(jnp.float32).astype(jnp.bfloat16)
    middle_lane = lane_iota(half_rows)
    edge_lane = lane_iota(BL)

    def one_box(inner, carry):
        box = pl.program_id(0) * PACK_BOXES + inner
        for slot in range(SLOTS):
            chunk = next(k for k, (at, n) in enumerate(CHUNKS) if at <= slot < at + n)
            put = functools.partial(out_refs[chunk].__setitem__)
            place = slot - CHUNKS[chunk][0]
            held = box * SLOTS + slot
            right = []
            for p in range(NB):
                rows = min(SR, (p + 1) * BL) - p * BL
                parts = []
                for half in range(2):
                    mask = jnp.where(
                        low_half,
                        pattern_ref[p, 2 * half, held].astype(jnp.float32),
                        pattern_ref[p, 2 * half + 1, held].astype(jnp.float32),
                    ).astype(jnp.bfloat16)
                    value = (
                        jac_ref[inner, slot, p * BL : p * BL + rows, half * LANES : (half + 1) * LANES]
                        * mask
                    )
                    parts.append(value * inside if p == NB - 1 else value)
                put((inner, place, slice(p * BL, p * BL + rows), slice(None)), parts[0])
                right.append(parts[1])
            upper = jnp.concatenate([right[0], right[1][: half_rows - BL]], axis=0)
            lower = jnp.concatenate([right[1][half_rows - BL :], right[2], right[3]], axis=0)
            middle = jnp.where(middle_lane < BL, upper, pltpu.roll(lower, BL, 1))
            put((inner, place, slice(SR, SR + half_rows), slice(None)), middle)
            last = jnp.concatenate([right[3], jnp.zeros((BL - tail, LANES), jnp.bfloat16)], axis=0)
            edge = jnp.where(
                edge_lane < 64,
                jnp.where(edge_lane < 32, pltpu.roll(right[0], 64, 1), pltpu.roll(right[1], 96, 1)),
                jnp.where(edge_lane < 96, right[2], pltpu.roll(last, 32, 1)),
            )
            put((inner, place, slice(SR + half_rows, PACK), slice(None)), edge)
        return carry

    lax.fori_loop(0, PACK_BOXES, one_box, 0)


def pack_all(jacobian, pattern, table, counts, diffusivity, cells):
    boxes = jacobian.shape[0]
    tiles = cells.shape[1]
    last = (S - 1) // TURN_SPECIES
    return pl.pallas_call(
        pack_kernel,
        grid=(boxes // PACK_BOXES,),
        in_specs=[
            pl.BlockSpec(memory_space=pltpu.SMEM),
            pl.BlockSpec(table.shape, lambda b: (0, 0)),
            pl.BlockSpec(counts.shape, lambda b: (0, 0)),
            pl.BlockSpec(diffusivity.shape, lambda b: (0, 0)),
            pl.BlockSpec(
                (TURN_SPECIES, tiles, LANES), lambda b: (jnp.minimum(b, last), 0, 0)
            ),
            pl.BlockSpec((PACK_BOXES, SLOTS, SR, SP), lambda b: (b, 0, 0, 0)),
        ],
        out_specs=[
            pl.BlockSpec((8, LANES), lambda b: (0, 0)),
            pl.BlockSpec((SR, LANES), lambda b: (0, 0)),
            pl.BlockSpec(
                (TURN_SPECIES, tiles, LANES), lambda b: (jnp.minimum(b, last), 0, 0)
            ),
        ]
        + [
            pl.BlockSpec((PACK_BOXES, n, PACK, LANES), lambda b: (b, 0, 0, 0)) for _, n in CHUNKS
        ],
        out_shape=[
            jax.ShapeDtypeStruct((8, LANES), jnp.int32),
            jax.ShapeDtypeStruct((SR, LANES), jnp.float32),
            jax.ShapeDtypeStruct((S, tiles, LANES), jnp.float32),
        ]
        + [
            jax.ShapeDtypeStruct((boxes, n, PACK, LANES), jnp.bfloat16) for _, n in CHUNKS
        ],
        compiler_params=pltpu.CompilerParams(vmem_limit_bytes=WIDE_VMEM),
        name="pack_all",
    )(pattern, table, counts, diffusivity, cells, jacobian)


def unpack(packed_ref, item, dense_ref):
    half_rows = SR // 2
    dense_ref[:, 0:LANES] = packed_ref[item, pl.ds(0, SR), :]
    middle = packed_ref[item, pl.ds(SR, half_rows), :]
    edge = packed_ref[item, pl.ds(SR + half_rows, BL), :]
    high = pltpu.roll(middle, BL, 1)

    def put(row, rows, low, rest):
        dense_ref[pl.ds(row, rows), LANES:SP] = jnp.where(lane_iota(rows) < BL, low, rest)

    put(0, 64, middle[0:64], pltpu.roll(edge, 64, 1))
    shifted = pltpu.roll(edge, 32, 1)
    put(64, 48, middle[64:112], shifted[0:48])
    put(112, 16, high[0:16], shifted[48:64])
    put(128, 64, high[16:80], edge)
    put(192, 32, high[80:112], pltpu.roll(edge[0:32], 96, 1))


def solve_kernel(chunk, *refs):
    if chunk == 0:
        plan_ref, state_hbm, packed_hbm, out_hbm, rows_hbm, edge_ref = refs[:6]
        scratch = refs[6:]
    else:
        plan_ref, state_hbm, packed_hbm, second_hbm, _, _, edge_in = refs[:7]
        out_hbm, rows_hbm, edge_ref = refs[7:10]
        scratch = refs[10:]
    packed, state, outgoing, arrived, sent = scratch[:5]
    dense, right, left_over, mapped, guess, sums = (
        scratch[5 + GROUP * kind : 5 + GROUP * (kind + 1)] for kind in range(6)
    )
    tiles = state_hbm.shape[1]
    begun = plan_ref[3, 0]
    base = 0 if chunk == 0 else begun
    groups = (begun if chunk == 0 else tiles - begun) // GROUP

    def fetch(place, origin, at):
        return pltpu.make_async_copy(origin.at[at], packed.at[place], arrived.at[0, place])

    def fetch_state(place):
        tile = plan_ref[1, base + place]
        return pltpu.make_async_copy(
            state_hbm.at[:, tile, :], state.at[place, 0:S], arrived.at[1, place]
        )

    def start_fetch(place, carry):
        at = plan_ref[0, base + place]
        state[place, SR - 8 : SR, :] = jnp.zeros((8, LANES), jnp.float32)
        fetch_state(place).start()
        if chunk == 0:
            fetch(place, packed_hbm, at).start()
        else:
            early = packed_hbm.shape[0]

            @pl.when(at < early)
            def _():
                fetch(place, packed_hbm, at).start()

            @pl.when(at >= early)
            def _():
                fetch(place, second_hbm, at - early).start()

        return carry

    lax.fori_loop(0, groups * GROUP, start_fetch, 0)
    for member in range(GROUP):
        right[member][SR:SP, :] = jnp.zeros((SP - SR, SP), jnp.bfloat16)
    if chunk == 0:
        edge_ref[...] = jnp.zeros_like(edge_ref)
    else:
        edge_ref[...] = edge_in[...]
    edge_lane = lane_iota(SR) // 4

    def send(buffer, member, tile):
        return pltpu.make_async_copy(
            outgoing.at[buffer, member], out_hbm.at[tile], sent.at[buffer, member]
        )

    def send_row(buffer, member, tile):
        at = jnp.where(tile < 2, tile, tile - (tiles - 4))
        return pltpu.make_async_copy(
            outgoing.at[buffer, member], rows_hbm.at[at], sent.at[2 + buffer, member]
        )

    def is_row(tile):
        return (tile < 2) | (tile >= tiles - 2)

    def drain(group_no):
        for member in range(GROUP):
            tile = plan_ref[1, base + group_no * GROUP + member]
            send(group_no % 2, member, tile).wait()

            @pl.when(is_row(tile))
            def _():
                send_row(group_no % 2, member, tile).wait()

    def split(member, row, rows, remainder):
        high = remainder.astype(jnp.bfloat16)
        span = slice(row, row + rows)
        right[member][span, 0:LANES] = high
        right[member][span, LANES:SP] = (remainder - high.astype(jnp.float32)).astype(
            jnp.bfloat16
        )

    def multiply(member):
        return jnp.dot(
            dense[member][...], right[member][...], preferred_element_type=jnp.float32
        )

    def measure(member, product):
        above = jnp.zeros((8, LANES), jnp.float32)
        below = jnp.zeros((8, LANES), jnp.float32)
        for row in range(0, SR, 8):
            span = slice(row, row + 8)
            remainder = left_over[member][span, :]
            value = remainder - (product[span, 0:LANES] + product[span, LANES:SP])
            mapped[member][span, :] = value
            above = above + remainder * value
            below = below + value * value
        return above, below

    def move(member, above, below, active):
        above = jnp.sum(above, axis=0, keepdims=True)
        below = jnp.sum(below, axis=0, keepdims=True) + EPSILON
        step = jnp.where(active, above / below, 0.0)
        for row in range(0, SR, 16):
            span = slice(row, row + 16)
            remainder = left_over[member][span, :]
            guess[member][span, :] += step * remainder
            remainder = remainder - step * mapped[member][span, :]
            left_over[member][span, :] = remainder
            split(member, row, 16, remainder)

    def keep_sums(member, above, below):
        sums[member][0:8, :] = above
        sums[member][8:16, :] = below

    def one_group(group_no, carry):
        buffer = group_no % 2
        places = [group_no * GROUP + member for member in range(GROUP)]
        chosen = [plan_ref[1, base + place] for place in places]
        counts = [plan_ref[2, base + place] for place in places]

        for member in range(GROUP):
            fetch(places[member], packed_hbm, 0).wait()
            fetch_state(places[member]).wait()
        for member in range(GROUP):
            unpack(packed, places[member], dense[member])
            start_value = state[places[member]]
            right[member][0:SR, 0:LANES] = start_value.astype(jnp.bfloat16)
            guess[member][...] = start_value
        for member in range(GROUP):
            remainder = jnp.dot(
                dense[member][...],
                right[member][:, 0:LANES],
                preferred_element_type=jnp.float32,
            )
            left_over[member][...] = remainder
            split(member, 0, SR, remainder)

        half = GROUP // 2
        for member in range(half, GROUP):
            keep_sums(member, *measure(member, multiply(member)))

        def advance(turn_no, inner):
            for one, other in zip(range(half), range(half, GROUP)):
                product = multiply(one)
                move(other, sums[other][0:8, :], sums[other][8:16, :], turn_no < counts[other])
                next_product = multiply(other)
                move(one, *measure(one, product), turn_no < counts[one])
                keep_sums(other, *measure(other, next_product))
            return inner

        lax.fori_loop(0, functools.reduce(jnp.maximum, counts), advance, 0)

        @pl.when(group_no >= 2)
        def _():
            drain(group_no - 2)

        for member in range(GROUP):
            result = guess[member][...]
            outgoing[buffer, member] = result
            tile = chosen[member]
            edge_ref[...] = jnp.where(
                edge_lane == tile, pltpu.roll(result, (4 * tile + 2) % LANES, 1), edge_ref[...]
            )
            send(buffer, member, tile).start()

            @pl.when(is_row(tile))
            def _():
                send_row(buffer, member, tile).start()

        return carry

    lax.fori_loop(0, groups, one_group, 0)

    for back in range(2):
        @pl.when(groups > back)
        def _():
            drain(groups - 1 - back)

    edge_ref[S + 2 : SR, :] = jnp.ones((SR - S - 2, LANES), jnp.float32)


def solve_chunk(chunk, plan, state, packed, reacted, rows, edge):
    tiles = state.shape[1]
    out_shape = (
        jax.ShapeDtypeStruct((tiles, SR, LANES), jnp.float32),
        jax.ShapeDtypeStruct((4, SR, LANES), jnp.float32),
        jax.ShapeDtypeStruct((SR, LANES), jnp.float32),
    )
    anywhere = pl.BlockSpec(memory_space=pl.ANY)
    vmem = pl.BlockSpec(memory_space=pltpu.VMEM)
    in_specs = [pl.BlockSpec(memory_space=pltpu.SMEM), anywhere]
    in_specs += [anywhere] * (chunk + 1)
    operands = [plan, state, *packed[: chunk + 1]]
    aliases = {}
    if chunk:
        in_specs += [anywhere, anywhere, vmem]
        operands += [reacted, rows, edge]
        aliases = {4: 0, 5: 1}
    tile_values = pltpu.VMEM((SR, LANES), jnp.float32)
    return pl.pallas_call(
        functools.partial(solve_kernel, chunk),
        in_specs=in_specs,
        out_specs=(anywhere, anywhere, vmem),
        out_shape=out_shape,
        input_output_aliases=aliases,
        scratch_shapes=[
            pltpu.VMEM((tiles, PACK, LANES), jnp.bfloat16),
            pltpu.VMEM((tiles, SR, LANES), jnp.float32),
            pltpu.VMEM((2, GROUP, SR, LANES), jnp.float32),
            pltpu.SemaphoreType.DMA((2, tiles)),
            pltpu.SemaphoreType.DMA((4, GROUP)),
        ]
        + [pltpu.VMEM((SR, SP), jnp.bfloat16)] * GROUP
        + [pltpu.VMEM((SP, SP), jnp.bfloat16)] * GROUP
        + [tile_values] * (3 * GROUP)
        + [pltpu.VMEM((16, LANES), jnp.float32)] * GROUP,
        compiler_params=pltpu.CompilerParams(vmem_limit_bytes=WIDE_VMEM),
        cost_estimate=pl.CostEstimate(
            flops=16 * 300_000_000, bytes_accessed=16 * 200000, transcendentals=0
        ),
        name="solve_chunk",
    )(*operands)


def message_kernel(rows_ref, low_ref, high_ref, down_ref, up_ref):
    tiles = LANES // 4
    down_ref[0:2] = rows_ref[2:4].astype(jnp.bfloat16)
    up_ref[0:2] = rows_ref[0:2].astype(jnp.bfloat16)
    lanes = lane_iota(SR)
    for row, out_ref in ((tiles - 1, down_ref), (0, up_ref)):
        cells = jnp.where(
            lanes == 0,
            pltpu.roll(low_ref[...], (-(4 * row + 1)) % LANES, 1),
            pltpu.roll(high_ref[...], (-(4 * row + 3)) % LANES, 1),
        )
        out_ref[2] = jnp.where(lanes == 2, 1.0, cells).astype(jnp.bfloat16)


def make_messages(rows, low, high):
    vmem = pl.BlockSpec(memory_space=pltpu.VMEM)
    shape = jax.ShapeDtypeStruct((3, SR, LANES), jnp.bfloat16)
    return pl.pallas_call(
        message_kernel,
        in_specs=[vmem, vmem, vmem],
        out_specs=(vmem, vmem),
        out_shape=(shape, shape),
        compiler_params=pltpu.CompilerParams(vmem_limit_bytes=TIGHT_VMEM),
        name="make_messages",
    )(rows, low, high)


def beside(value, lanes):
    return jnp.where(lanes == 0, 0.0, pltpu.roll(value, 1, 1)) + jnp.where(
        lanes == LANES - 1, 0.0, pltpu.roll(value, LANES - 1, 1)
    )


def inner_kernel(tiles, block_ref, rate_ref, both_ref, out_ref):
    zero = jnp.zeros((1, 8, LANES), jnp.float32)

    def around(value, by):
        gap = jnp.concatenate([zero] * by, axis=0)
        return jnp.concatenate([gap, value[: tiles - by]], axis=0) + jnp.concatenate(
            [value[by:], gap], axis=0
        )

    for number in range(SPECIES // 8):
        span = slice(number * 8, number * 8 + 8)
        rate = rate_ref[span, :]
        keep = 1.0 - 4.0 * rate
        square = rate * rate
        cells = block_ref[:, span, :]
        flat = cells.reshape(tiles * 8, LANES)
        high = flat.astype(jnp.bfloat16)
        low = (flat - high.astype(jnp.float32)).astype(jnp.bfloat16)
        product = jnp.dot(
            jnp.concatenate([high, low], axis=1), both_ref[...], preferred_element_type=jnp.float32
        )
        once = product[:, 0:LANES].reshape(tiles, 8, LANES)
        twice = product[:, LANES:].reshape(tiles, 8, LANES)
        near = (2.0 * keep * rate) * (around(cells, 1) + once)
        sides = around(once, 1)
        far = square * ((around(cells, 2) + twice) + (sides + sides))
        own = keep * keep + 2.0 * square
        end = keep * keep + square
        value = near + far
        out_ref[1 : tiles - 1, span, :] = value[1 : tiles - 1] + own * cells[1 : tiles - 1]
        out_ref[0, span, :] = value[0] + end * cells[0]
        out_ref[tiles - 1, span, :] = value[tiles - 1] + end * cells[tiles - 1]


def diffuse_inside(block, rate):
    tiles = block.shape[0]
    cells = pl.BlockSpec((tiles, SPECIES, LANES), lambda g: (0, g, 0))
    place = np.arange(LANES)
    next_to = (np.abs(place[:, None] - place[None, :]) == 1).astype(np.float32)
    both = np.concatenate([next_to, next_to @ next_to], axis=1)
    both = jnp.asarray(np.concatenate([both, both], axis=0), jnp.bfloat16)
    return pl.pallas_call(
        functools.partial(inner_kernel, tiles),
        grid=(SR // SPECIES,),
        in_specs=[
            cells,
            pl.BlockSpec((SPECIES, LANES), lambda g: (g, 0)),
            pl.BlockSpec((2 * LANES, 2 * LANES), lambda g: (0, 0)),
        ],
        out_specs=cells,
        out_shape=jax.ShapeDtypeStruct(block.shape, jnp.float32),
        compiler_params=pltpu.CompilerParams(vmem_limit_bytes=INNER_VMEM),
        cost_estimate=pl.CostEstimate(
            flops=tiles * SR * LANES * 20, bytes_accessed=8 * block.size, transcendentals=0
        ),
        name="diffuse_inside",
    )(block, rate, both)


def border_kernel(tiles, inner_ref, top_ref, bottom_ref, above_ref, below_ref, low_ref, high_ref,
                  low_here_ref, high_here_ref, own_ref, rate_ref, out_ref):
    lanes = lane_iota(8)
    column = lanes % 4
    here = S + 2 - (SR - 8)
    has_side = jnp.where(
        column < 2, low_here_ref[here : here + 1, :], high_here_ref[here : here + 1, :]
    )
    near_edge = (lanes < 2) | (lanes >= LANES - 2)

    def slab(number):
        span = slice(number * 8, number * 8 + 8)
        overall = pl.program_id(0) * (SPECIES // 8) + number
        wide = pl.ds(pl.multiple_of(overall // 2 * 16, 16), 16)

        def read(ref, row):
            both = ref[row, wide, :].astype(jnp.float32)
            return jnp.where(overall % 2 == 0, both[0:8], both[8:16])

        rate = rate_ref[span, :]
        keep = 1.0 - 4.0 * rate
        own = own_ref[span, :]
        ghost = jnp.where(column < 2, low_ref[span, :], high_ref[span, :])

        def rows_beside(near, far, inner, corner):
            exists = jnp.broadcast_to(corner[:, 2:3], (8, LANES))
            left = jnp.where(lanes == 0, corner, pltpu.roll(near, 1, 1))
            right = jnp.where(lanes == LANES - 1, corner, pltpu.roll(near, LANES - 1, 1))
            later = (keep * near + rate * ((far + inner) + (left + right))) * exists
            first = rate * near
            outer = keep * first + rate * (beside(first, lanes) + later)
            return outer, rate * first

        corner_above, corner_below = read(above_ref, 2), read(below_ref, 2)
        row_terms = {}
        row_terms[0], row_terms[1] = rows_beside(
            read(above_ref, 1), read(above_ref, 0), top_ref[0, span, :], corner_above
        )
        row_terms[tiles - 1], row_terms[tiles - 2] = rows_beside(
            read(below_ref, 0), read(below_ref, 1), bottom_ref[0, span, :], corner_below
        )

        up = pltpu.roll(ghost, 4, 1)
        up = jnp.where(lanes == 1, pltpu.roll(corner_above, 1, 1), up)
        up = jnp.where(lanes == 2, pltpu.roll(corner_above, 3, 1), up)
        down = pltpu.roll(ghost, LANES - 4, 1)
        down = jnp.where(lanes == LANES - 3, pltpu.roll(corner_below, LANES - 3, 1), down)
        down = jnp.where(lanes == LANES - 2, pltpu.roll(corner_below, LANES - 1, 1), down)
        side = jnp.where(
            column == 1,
            pltpu.roll(own, LANES - 1, 1) + pltpu.roll(ghost, 1, 1),
            pltpu.roll(own, 1, 1) + pltpu.roll(ghost, LANES - 1, 1),
        )
        later = (keep * ghost + rate * ((up + down) + side)) * has_side
        first = rate * ghost
        first_up = jnp.where(lanes < 4, 0.0, pltpu.roll(first, 4, 1))
        first_down = jnp.where(lanes >= LANES - 4, 0.0, pltpu.roll(first, LANES - 4, 1))
        outer = keep * first + rate * ((first_up + first_down) + later)
        second = rate * first
        terms = jnp.where(
            column < 2,
            jnp.where(column == 0, pltpu.roll(second, LANES - 2, 1), pltpu.roll(outer, LANES - 1, 1)),
            jnp.where(column == 2, pltpu.roll(outer, 1, 1), pltpu.roll(second, 2, 1)),
        )
        values = []
        for row in range(tiles):
            value = inner_ref[row, span, :] + jnp.where(
                near_edge, pltpu.roll(terms, (-(4 * row + 2)) % LANES, 1), 0.0
            )
            if row in row_terms:
                value = value + row_terms[row]
            values.append(value)
        out_ref[span, :, :] = jnp.swapaxes(jnp.stack(values, axis=0), 0, 1)

    for number in range(SPECIES // 8):
        slab(number)


def add_borders(inner, rows, above, below, low, high, own, rate):
    tiles = inner.shape[0]
    message = pl.BlockSpec((3, SR, LANES), lambda g: (0, 0, 0))
    edge = pl.BlockSpec((SPECIES, LANES), lambda g: (g, 0))
    flags = pl.BlockSpec((8, LANES), lambda g: (SR // 8 - 1, 0))
    return pl.pallas_call(
        functools.partial(border_kernel, tiles),
        grid=(SR // SPECIES,),
        in_specs=[
            pl.BlockSpec((tiles, SPECIES, LANES), lambda g: (0, g, 0)),
            pl.BlockSpec((1, SPECIES, LANES), lambda g: (0, g, 0)),
            pl.BlockSpec((1, SPECIES, LANES), lambda g: (3, g, 0)),
            message,
            message,
            edge,
            edge,
            flags,
            flags,
            edge,
            edge,
        ],
        out_specs=pl.BlockSpec((SPECIES, tiles, LANES), lambda g: (g, 0, 0)),
        out_shape=jax.ShapeDtypeStruct((S, tiles, LANES), jnp.float32),
        compiler_params=pltpu.CompilerParams(vmem_limit_bytes=TIGHT_VMEM),
        name="add_borders",
    )(inner, rows, rows, above, below, low, high, low, high, own, rate)


def shifted(value, axis, by):
    count = lax.axis_size(axis)
    pairs = [(i, i + by) for i in range(count) if 0 <= i + by < count]
    return lax.ppermute(value, axis, pairs)


def on_device(species_state, stiffness, send_list, jacobian, pattern, diffusivity):
    boxes = lax.axis_size("box")
    tiles = species_state.shape[0]
    slots = jacobian.shape[0] // boxes
    by_box = jacobian.reshape(boxes, slots, SP, SP)
    counts = stiffness.reshape(1, tiles)
    table = send_list.transpose(0, 1, 3, 2).reshape(slots, boxes)
    by_block = pattern.transpose(1, 2, 3, 0).reshape(NB, NB, boxes * slots)
    plan, rate, state, first, second = pack_all(
        by_box, by_block, table, counts, diffusivity.reshape(1, S), species_state.transpose(1, 0, 2)
    )
    plan, rate, state, first, second = lax.optimization_barrier(
        (plan, rate, state, first, second)
    )

    def exchange(packed):
        arrived = lax.all_to_all(packed, "box", split_axis=0, concat_axis=0, tiled=True)
        return arrived.reshape(-1, PACK, LANES)

    first = exchange(first)
    plan, rate, state, first, second = lax.optimization_barrier(
        (plan, rate, state, first, second)
    )
    second = exchange(second)
    early, rows, edge = solve_chunk(0, plan, state, (first, second), None, None, None)
    reacted, rows, edge = solve_chunk(1, plan, state, (first, second), early, rows, edge)

    low = shifted(edge, "bal", 1)
    high = shifted(edge, "bal", -1)
    down, up = make_messages(rows, low, high)
    above = shifted(down, "box", 1)
    below = shifted(up, "box", -1)
    inner = diffuse_inside(reacted, rate)
    field = add_borders(inner, rows, above, below, low, high, edge, rate)
    return field.transpose(1, 0, 2)


def solution(mesh):
    in_specs = (
        P("box", None, "bal"),
        P("box", "bal"),
        P("box", "bal", None, None),
        P("box", "bal", None, None),
        P("box", "bal", None, None),
        P(),
    )
    return jax.shard_map(
        on_device,
        mesh=mesh,
        in_specs=in_specs,
        out_specs=P("box", None, "bal"),
        check_vma=False,
    )
```

```python
import functools

import jax
import numpy as np
import jax.numpy as jnp
from jax import lax
from jax.experimental import pallas as pl
from jax.experimental.pallas import tpu as pltpu
from jax.sharding import PartitionSpec as P

S = 218
SR = 224
SP = 256
BL = 64
NB = 4
PACK = 400
LANES = 128
EPSILON = 1e-06
GROUP = 8
SLOTS = 4
CHUNKS = ((0, 3), (3, 1))
PACK_BOXES = 8
TURN_SPECIES = 112
SPECIES = 56
WIDE_VMEM = 61 * 1024 * 1024
INNER_VMEM = 48 * 1024 * 1024
TIGHT_VMEM = 40 * 1024 * 1024


def lane_iota(rows):
    return lax.broadcasted_iota(jnp.int32, (rows, LANES), 1)


def make_plan(table, counts):
    slots, boxes = table.shape
    tiles = counts.shape[1]
    size = float(LANES)
    filler = jnp.full((slots, LANES - boxes), -1.0, jnp.float32)
    spread = jnp.concatenate([table.astype(jnp.float32), filler], axis=1)
    counts = jnp.concatenate(
        [counts.astype(jnp.float32), jnp.zeros((1, LANES - tiles), jnp.float32)], axis=1
    )
    lane = lane_iota(LANES).astype(jnp.float32)
    item = lax.broadcasted_iota(jnp.int32, (LANES, LANES), 0).astype(jnp.float32)
    row = jnp.full((1, LANES), -1.0, jnp.float32)
    for slot in range(slots):
        part = pltpu.roll(spread, slot * boxes, 1)[slot : slot + 1] if slot else spread[0:1]
        here = (lane_iota(1) >= slot * boxes) & (lane_iota(1) < (slot + 1) * boxes)
        row = jnp.where(here, part, row)
    tile = jnp.transpose(jnp.broadcast_to(row, (LANES, LANES)))
    turns = jnp.sum(jnp.where(tile == lane, counts, 0.0), axis=1, keepdims=True)
    turns = jnp.broadcast_to(turns, (LANES, LANES))
    live = tile >= 0.0
    early_size = CHUNKS[0][1] * boxes
    early = live & (item < early_size)
    weight = (size - turns) * size + item

    def rank(key):
        smaller = jnp.where(jnp.transpose(key) < key, 1.0, 0.0)
        return jnp.broadcast_to(jnp.sum(smaller, axis=1, keepdims=True), (LANES, LANES))

    late = 4.0 * size * size
    begun = jnp.sum(jnp.where(early, 1.0, 0.0), axis=0, keepdims=True)
    begun = jnp.floor(begun * (1.0 / GROUP)) * GROUP
    chosen = early & (rank(jnp.where(early, weight, late + item)) < begun)
    place = rank(weight + jnp.where(chosen, 0.0, jnp.where(live, late, 2.0 * late)))
    slot_of = jnp.floor(item * (1.0 / boxes))
    box_of = item - slot_of * boxes
    width = float(CHUNKS[0][1])
    source = jnp.where(item < early_size, box_of * width + slot_of, item)
    rows = [
        jnp.sum(jnp.where(place == lane, value, 0.0), axis=0, keepdims=True)
        for value in (source, tile, turns)
    ]
    rows += [begun, jnp.zeros((4, LANES), jnp.float32)]
    return jnp.concatenate(rows, axis=0).astype(jnp.int32)


def pack_kernel(pattern_ref, table_ref, counts_ref, diffusivity_ref, cells_ref, jac_ref,
                plan_ref, rate_ref, state_ref, *out_refs):
    @pl.when(pl.program_id(0) == 0)
    def _():
        plan_ref[...] = make_plan(table_ref[...], counts_ref[...])
        row = jnp.concatenate(
            [diffusivity_ref[...], jnp.zeros((1, SP - S), jnp.float32)], axis=1
        )
        for start in (0, LANES):
            rows = min(LANES, SR - start)
            part = jnp.broadcast_to(row[:, start : start + LANES], (LANES, LANES))
            rate_ref[start : start + rows, :] = jnp.transpose(part)[0:rows]

    state_ref[...] = cells_ref[...].astype(jnp.float32)

    low_half = lane_iota(1) < BL
    half_rows = SR // 2
    tail = SR - (NB - 1) * BL
    inside = lax.broadcasted_iota(jnp.int32, (tail, LANES), 0) < S - (NB - 1) * BL
    inside = inside.astype(jnp.float32).astype(jnp.bfloat16)
    middle_lane = lane_iota(half_rows)
    edge_lane = lane_iota(BL)

    def one_box(inner, carry):
        box = pl.program_id(0) * PACK_BOXES + inner
        for slot in range(SLOTS):
            chunk = next(k for k, (at, n) in enumerate(CHUNKS) if at <= slot < at + n)
            put = functools.partial(out_refs[chunk].__setitem__)
            place = slot - CHUNKS[chunk][0]
            held = box * SLOTS + slot
            right = []
            for p in range(NB):
                rows = min(SR, (p + 1) * BL) - p * BL
                parts = []
                for half in range(2):
                    mask = jnp.where(
                        low_half,
                        pattern_ref[p, 2 * half, held].astype(jnp.float32),
                        pattern_ref[p, 2 * half + 1, held].astype(jnp.float32),
                    ).astype(jnp.bfloat16)
                    value = (
                        jac_ref[inner, slot, p * BL : p * BL + rows, half * LANES : (half + 1) * LANES]
                        * mask
                    )
                    parts.append(value * inside if p == NB - 1 else value)
                put((inner, place, slice(p * BL, p * BL + rows), slice(None)), parts[0])
                right.append(parts[1])
            upper = jnp.concatenate([right[0], right[1][: half_rows - BL]], axis=0)
            lower = jnp.concatenate([right[1][half_rows - BL :], right[2], right[3]], axis=0)
            middle = jnp.where(middle_lane < BL, upper, pltpu.roll(lower, BL, 1))
            put((inner, place, slice(SR, SR + half_rows), slice(None)), middle)
            last = jnp.concatenate([right[3], jnp.zeros((BL - tail, LANES), jnp.bfloat16)], axis=0)
            edge = jnp.where(
                edge_lane < 64,
                jnp.where(edge_lane < 32, pltpu.roll(right[0], 64, 1), pltpu.roll(right[1], 96, 1)),
                jnp.where(edge_lane < 96, right[2], pltpu.roll(last, 32, 1)),
            )
            put((inner, place, slice(SR + half_rows, PACK), slice(None)), edge)
        return carry

    lax.fori_loop(0, PACK_BOXES, one_box, 0)


def pack_all(jacobian, pattern, table, counts, diffusivity, cells):
    boxes = jacobian.shape[0]
    tiles = cells.shape[1]
    last = (S - 1) // TURN_SPECIES
    return pl.pallas_call(
        pack_kernel,
        grid=(boxes // PACK_BOXES,),
        in_specs=[
            pl.BlockSpec(memory_space=pltpu.SMEM),
            pl.BlockSpec(table.shape, lambda b: (0, 0)),
            pl.BlockSpec(counts.shape, lambda b: (0, 0)),
            pl.BlockSpec(diffusivity.shape, lambda b: (0, 0)),
            pl.BlockSpec(
                (TURN_SPECIES, tiles, LANES), lambda b: (jnp.minimum(b, last), 0, 0)
            ),
            pl.BlockSpec((PACK_BOXES, SLOTS, SR, SP), lambda b: (b, 0, 0, 0)),
        ],
        out_specs=[
            pl.BlockSpec((8, LANES), lambda b: (0, 0)),
            pl.BlockSpec((SR, LANES), lambda b: (0, 0)),
            pl.BlockSpec(
                (TURN_SPECIES, tiles, LANES), lambda b: (jnp.minimum(b, last), 0, 0)
            ),
        ]
        + [
            pl.BlockSpec((PACK_BOXES, n, PACK, LANES), lambda b: (b, 0, 0, 0)) for _, n in CHUNKS
        ],
        out_shape=[
            jax.ShapeDtypeStruct((8, LANES), jnp.int32),
            jax.ShapeDtypeStruct((SR, LANES), jnp.float32),
            jax.ShapeDtypeStruct((S, tiles, LANES), jnp.float32),
        ]
        + [
            jax.ShapeDtypeStruct((boxes, n, PACK, LANES), jnp.bfloat16) for _, n in CHUNKS
        ],
        compiler_params=pltpu.CompilerParams(vmem_limit_bytes=WIDE_VMEM),
        name="pack_all",
    )(pattern, table, counts, diffusivity, cells, jacobian)


def unpack(packed_ref, item, dense_ref):
    half_rows = SR // 2
    dense_ref[:, 0:LANES] = packed_ref[item, pl.ds(0, SR), :]
    middle = packed_ref[item, pl.ds(SR, half_rows), :]
    edge = packed_ref[item, pl.ds(SR + half_rows, BL), :]
    high = pltpu.roll(middle, BL, 1)

    def put(row, rows, low, rest):
        dense_ref[pl.ds(row, rows), LANES:SP] = jnp.where(lane_iota(rows) < BL, low, rest)

    put(0, 64, middle[0:64], pltpu.roll(edge, 64, 1))
    shifted = pltpu.roll(edge, 32, 1)
    put(64, 48, middle[64:112], shifted[0:48])
    put(112, 16, high[0:16], shifted[48:64])
    put(128, 64, high[16:80], edge)
    put(192, 32, high[80:112], pltpu.roll(edge[0:32], 96, 1))


def solve_kernel(chunk, *refs):
    if chunk == 0:
        plan_ref, state_hbm, packed_hbm, out_hbm, rows_hbm, edge_ref = refs[:6]
        scratch = refs[6:]
    else:
        plan_ref, state_hbm, packed_hbm, second_hbm, _, _, edge_in = refs[:7]
        out_hbm, rows_hbm, edge_ref = refs[7:10]
        scratch = refs[10:]
    packed, state, outgoing, arrived, sent = scratch[:5]
    dense, right, left_over, mapped, guess, sums = (
        scratch[5 + GROUP * kind : 5 + GROUP * (kind + 1)] for kind in range(6)
    )
    tiles = state_hbm.shape[1]
    begun = plan_ref[3, 0]
    base = 0 if chunk == 0 else begun
    groups = (begun if chunk == 0 else tiles - begun) // GROUP

    def fetch(place, origin, at):
        return pltpu.make_async_copy(origin.at[at], packed.at[place], arrived.at[0, place])

    def fetch_state(place):
        tile = plan_ref[1, base + place]
        return pltpu.make_async_copy(
            state_hbm.at[:, tile, :], state.at[place, 0:S], arrived.at[1, place]
        )

    def start_fetch(place, carry):
        at = plan_ref[0, base + place]
        state[place, SR - 8 : SR, :] = jnp.zeros((8, LANES), jnp.float32)
        fetch_state(place).start()
        if chunk == 0:
            fetch(place, packed_hbm, at).start()
        else:
            early = packed_hbm.shape[0]

            @pl.when(at < early)
            def _():
                fetch(place, packed_hbm, at).start()

            @pl.when(at >= early)
            def _():
                fetch(place, second_hbm, at - early).start()

        return carry

    lax.fori_loop(0, groups * GROUP, start_fetch, 0)
    for member in range(GROUP):
        right[member][SR:SP, :] = jnp.zeros((SP - SR, SP), jnp.bfloat16)
    if chunk == 0:
        edge_ref[...] = jnp.zeros_like(edge_ref)
    else:
        edge_ref[...] = edge_in[...]
    edge_lane = lane_iota(SR) // 4

    def send(buffer, member, tile):
        return pltpu.make_async_copy(
            outgoing.at[buffer, member], out_hbm.at[tile], sent.at[buffer, member]
        )

    def send_row(buffer, member, tile):
        at = jnp.where(tile < 2, tile, tile - (tiles - 4))
        return pltpu.make_async_copy(
            outgoing.at[buffer, member], rows_hbm.at[at], sent.at[2 + buffer, member]
        )

    def is_row(tile):
        return (tile < 2) | (tile >= tiles - 2)

    def drain(group_no):
        for member in range(GROUP):
            tile = plan_ref[1, base + group_no * GROUP + member]
            send(group_no % 2, member, tile).wait()

            @pl.when(is_row(tile))
            def _():
                send_row(group_no % 2, member, tile).wait()

    def split(member, row, rows, remainder):
        high = remainder.astype(jnp.bfloat16)
        span = slice(row, row + rows)
        right[member][span, 0:LANES] = high
        right[member][span, LANES:SP] = (remainder - high.astype(jnp.float32)).astype(
            jnp.bfloat16
        )

    def multiply(member):
        return jnp.dot(
            dense[member][...], right[member][...], preferred_element_type=jnp.float32
        )

    def measure(member, product):
        above = jnp.zeros((8, LANES), jnp.float32)
        below = jnp.zeros((8, LANES), jnp.float32)
        for row in range(0, SR, 8):
            span = slice(row, row + 8)
            remainder = left_over[member][span, :]
            value = remainder - (product[span, 0:LANES] + product[span, LANES:SP])
            mapped[member][span, :] = value
            above = above + remainder * value
            below = below + value * value
        return above, below

    def move(member, above, below, active):
        above = jnp.sum(above, axis=0, keepdims=True)
        below = jnp.sum(below, axis=0, keepdims=True) + EPSILON
        step = jnp.where(active, above / below, 0.0)
        for row in range(0, SR, 16):
            span = slice(row, row + 16)
            remainder = left_over[member][span, :]
            guess[member][span, :] += step * remainder
            remainder = remainder - step * mapped[member][span, :]
            left_over[member][span, :] = remainder
            split(member, row, 16, remainder)

    def keep_sums(member, above, below):
        sums[member][0:8, :] = above
        sums[member][8:16, :] = below

    def one_group(group_no, carry):
        buffer = group_no % 2
        places = [group_no * GROUP + member for member in range(GROUP)]
        chosen = [plan_ref[1, base + place] for place in places]
        counts = [plan_ref[2, base + place] for place in places]

        for member in range(GROUP):
            fetch(places[member], packed_hbm, 0).wait()
            fetch_state(places[member]).wait()
        for member in range(GROUP):
            unpack(packed, places[member], dense[member])
            start_value = state[places[member]]
            right[member][0:SR, 0:LANES] = start_value.astype(jnp.bfloat16)
            guess[member][...] = start_value
        for member in range(GROUP):
            remainder = jnp.dot(
                dense[member][...],
                right[member][:, 0:LANES],
                preferred_element_type=jnp.float32,
            )
            left_over[member][...] = remainder
            split(member, 0, SR, remainder)

        half = GROUP // 2
        for member in range(half, GROUP):
            keep_sums(member, *measure(member, multiply(member)))

        def advance(turn_no, inner):
            for one, other in zip(range(half), range(half, GROUP)):
                product = multiply(one)
                move(other, sums[other][0:8, :], sums[other][8:16, :], turn_no < counts[other])
                next_product = multiply(other)
                move(one, *measure(one, product), turn_no < counts[one])
                keep_sums(other, *measure(other, next_product))
            return inner

        lax.fori_loop(0, functools.reduce(jnp.maximum, counts), advance, 0)

        @pl.when(group_no >= 2)
        def _():
            drain(group_no - 2)

        for member in range(GROUP):
            result = guess[member][...]
            outgoing[buffer, member] = result
            tile = chosen[member]
            edge_ref[...] = jnp.where(
                edge_lane == tile, pltpu.roll(result, (4 * tile + 2) % LANES, 1), edge_ref[...]
            )
            send(buffer, member, tile).start()

            @pl.when(is_row(tile))
            def _():
                send_row(buffer, member, tile).start()

        return carry

    lax.fori_loop(0, groups, one_group, 0)

    for back in range(2):
        @pl.when(groups > back)
        def _():
            drain(groups - 1 - back)

    edge_ref[S + 2 : SR, :] = jnp.ones((SR - S - 2, LANES), jnp.float32)


def solve_chunk(chunk, plan, state, packed, reacted, rows, edge):
    tiles = state.shape[1]
    out_shape = (
        jax.ShapeDtypeStruct((tiles, SR, LANES), jnp.float32),
        jax.ShapeDtypeStruct((4, SR, LANES), jnp.float32),
        jax.ShapeDtypeStruct((SR, LANES), jnp.float32),
    )
    anywhere = pl.BlockSpec(memory_space=pl.ANY)
    vmem = pl.BlockSpec(memory_space=pltpu.VMEM)
    in_specs = [pl.BlockSpec(memory_space=pltpu.SMEM), anywhere]
    in_specs += [anywhere] * (chunk + 1)
    operands = [plan, state, *packed[: chunk + 1]]
    aliases = {}
    if chunk:
        in_specs += [anywhere, anywhere, vmem]
        operands += [reacted, rows, edge]
        aliases = {4: 0, 5: 1}
    tile_values = pltpu.VMEM((SR, LANES), jnp.float32)
    return pl.pallas_call(
        functools.partial(solve_kernel, chunk),
        in_specs=in_specs,
        out_specs=(anywhere, anywhere, vmem),
        out_shape=out_shape,
        input_output_aliases=aliases,
        scratch_shapes=[
            pltpu.VMEM((tiles, PACK, LANES), jnp.bfloat16),
            pltpu.VMEM((tiles, SR, LANES), jnp.float32),
            pltpu.VMEM((2, GROUP, SR, LANES), jnp.float32),
            pltpu.SemaphoreType.DMA((2, tiles)),
            pltpu.SemaphoreType.DMA((4, GROUP)),
        ]
        + [pltpu.VMEM((SR, SP), jnp.bfloat16)] * GROUP
        + [pltpu.VMEM((SP, SP), jnp.bfloat16)] * GROUP
        + [tile_values] * (3 * GROUP)
        + [pltpu.VMEM((16, LANES), jnp.float32)] * GROUP,
        compiler_params=pltpu.CompilerParams(vmem_limit_bytes=WIDE_VMEM),
        cost_estimate=pl.CostEstimate(
            flops=16 * 300_000_000, bytes_accessed=16 * 200000, transcendentals=0
        ),
        name="solve_chunk",
    )(*operands)


def is_odd(axis):
    return lax.rem(lax.axis_index(axis), 2) == 1


def message_kernel(rows_ref, near_ref, far_ref, near_out_ref, far_out_ref):
    tiles = LANES // 4
    lanes = lane_iota(SR)
    odd = is_odd("bal")
    low = jnp.where(odd, near_ref[...], far_ref[...])
    high = jnp.where(odd, far_ref[...], near_ref[...])
    odd = is_odd("box")

    def message(start, row, near):
        for to_near, out_ref in ((near, near_out_ref), (jnp.logical_not(near), far_out_ref)):

            @pl.when(to_near)
            def _():
                out_ref[0:2] = rows_ref[start : start + 2].astype(jnp.bfloat16)
                cells = jnp.where(
                    lanes == 0,
                    pltpu.roll(low, (-(4 * row + 1)) % LANES, 1),
                    pltpu.roll(high, (-(4 * row + 3)) % LANES, 1),
                )
                out_ref[2] = jnp.where(lanes == 2, 1.0, cells).astype(jnp.bfloat16)

    message(0, 0, odd)
    message(2, tiles - 1, jnp.logical_not(odd))


def make_messages(rows, near, far):
    vmem = pl.BlockSpec(memory_space=pltpu.VMEM)
    shape = jax.ShapeDtypeStruct((3, SR, LANES), jnp.bfloat16)
    return pl.pallas_call(
        message_kernel,
        in_specs=[vmem, vmem, vmem],
        out_specs=(vmem, vmem),
        out_shape=(shape, shape),
        compiler_params=pltpu.CompilerParams(vmem_limit_bytes=TIGHT_VMEM),
        name="make_messages",
    )(rows, near, far)


def beside(value, lanes):
    return jnp.where(lanes == 0, 0.0, pltpu.roll(value, 1, 1)) + jnp.where(
        lanes == LANES - 1, 0.0, pltpu.roll(value, LANES - 1, 1)
    )


def inner_kernel(tiles, block_ref, rate_ref, both_ref, out_ref):
    zero = jnp.zeros((1, 8, LANES), jnp.float32)

    def around(value, by):
        gap = jnp.concatenate([zero] * by, axis=0)
        return jnp.concatenate([gap, value[: tiles - by]], axis=0) + jnp.concatenate(
            [value[by:], gap], axis=0
        )

    for number in range(SPECIES // 8):
        span = slice(number * 8, number * 8 + 8)
        rate = rate_ref[span, :]
        keep = 1.0 - 4.0 * rate
        square = rate * rate
        cells = block_ref[:, span, :]
        flat = cells.reshape(tiles * 8, LANES)
        high = flat.astype(jnp.bfloat16)
        low = (flat - high.astype(jnp.float32)).astype(jnp.bfloat16)
        product = jnp.dot(
            jnp.concatenate([high, low], axis=1), both_ref[...], preferred_element_type=jnp.float32
        )
        once = product[:, 0:LANES].reshape(tiles, 8, LANES)
        twice = product[:, LANES:].reshape(tiles, 8, LANES)
        near = (2.0 * keep * rate) * (around(cells, 1) + once)
        sides = around(once, 1)
        far = square * ((around(cells, 2) + twice) + (sides + sides))
        own = keep * keep + 2.0 * square
        end = keep * keep + square
        value = near + far
        out_ref[1 : tiles - 1, span, :] = value[1 : tiles - 1] + own * cells[1 : tiles - 1]
        out_ref[0, span, :] = value[0] + end * cells[0]
        out_ref[tiles - 1, span, :] = value[tiles - 1] + end * cells[tiles - 1]


def diffuse_inside(block, rate):
    tiles = block.shape[0]
    cells = pl.BlockSpec((tiles, SPECIES, LANES), lambda g: (0, g, 0))
    place = np.arange(LANES)
    next_to = (np.abs(place[:, None] - place[None, :]) == 1).astype(np.float32)
    both = np.concatenate([next_to, next_to @ next_to], axis=1)
    both = jnp.asarray(np.concatenate([both, both], axis=0), jnp.bfloat16)
    return pl.pallas_call(
        functools.partial(inner_kernel, tiles),
        grid=(SR // SPECIES,),
        in_specs=[
            cells,
            pl.BlockSpec((SPECIES, LANES), lambda g: (g, 0)),
            pl.BlockSpec((2 * LANES, 2 * LANES), lambda g: (0, 0)),
        ],
        out_specs=cells,
        out_shape=jax.ShapeDtypeStruct(block.shape, jnp.float32),
        compiler_params=pltpu.CompilerParams(vmem_limit_bytes=INNER_VMEM),
        cost_estimate=pl.CostEstimate(
            flops=tiles * SR * LANES * 20, bytes_accessed=8 * block.size, transcendentals=0
        ),
        name="diffuse_inside",
    )(block, rate, both)


def border_kernel(tiles, inner_ref, top_ref, bottom_ref, near_row_ref, far_row_ref, near_ref,
                  far_ref, near_here_ref, far_here_ref, own_ref, rate_ref, out_ref):
    lanes = lane_iota(8)
    column = lanes % 4
    here = S + 2 - (SR - 8)
    from_near = (column < 2) == is_odd("bal")
    near_above = is_odd("box")
    has_side = jnp.where(
        from_near, near_here_ref[here : here + 1, :], far_here_ref[here : here + 1, :]
    )
    near_edge = (lanes < 2) | (lanes >= LANES - 2)

    def slab(number):
        span = slice(number * 8, number * 8 + 8)
        overall = pl.program_id(0) * (SPECIES // 8) + number
        wide = pl.ds(pl.multiple_of(overall // 2 * 16, 16), 16)

        def read(ref, row):
            both = ref[row, wide, :].astype(jnp.float32)
            return jnp.where(overall % 2 == 0, both[0:8], both[8:16])

        near_rows = [read(near_row_ref, row) for row in range(3)]
        far_rows = [read(far_row_ref, row) for row in range(3)]
        above = [jnp.where(near_above, a, b) for a, b in zip(near_rows, far_rows)]
        below = [jnp.where(near_above, b, a) for a, b in zip(near_rows, far_rows)]

        rate = rate_ref[span, :]
        keep = 1.0 - 4.0 * rate
        own = own_ref[span, :]
        ghost = jnp.where(from_near, near_ref[span, :], far_ref[span, :])

        def rows_beside(near, far, inner, corner):
            exists = jnp.broadcast_to(corner[:, 2:3], (8, LANES))
            left = jnp.where(lanes == 0, corner, pltpu.roll(near, 1, 1))
            right = jnp.where(lanes == LANES - 1, corner, pltpu.roll(near, LANES - 1, 1))
            later = (keep * near + rate * ((far + inner) + (left + right))) * exists
            first = rate * near
            outer = keep * first + rate * (beside(first, lanes) + later)
            return outer, rate * first

        corner_above, corner_below = above[2], below[2]
        row_terms = {}
        row_terms[0], row_terms[1] = rows_beside(
            above[1], above[0], top_ref[0, span, :], corner_above
        )
        row_terms[tiles - 1], row_terms[tiles - 2] = rows_beside(
            below[0], below[1], bottom_ref[0, span, :], corner_below
        )

        up = pltpu.roll(ghost, 4, 1)
        up = jnp.where(lanes == 1, pltpu.roll(corner_above, 1, 1), up)
        up = jnp.where(lanes == 2, pltpu.roll(corner_above, 3, 1), up)
        down = pltpu.roll(ghost, LANES - 4, 1)
        down = jnp.where(lanes == LANES - 3, pltpu.roll(corner_below, LANES - 3, 1), down)
        down = jnp.where(lanes == LANES - 2, pltpu.roll(corner_below, LANES - 1, 1), down)
        side = jnp.where(
            column == 1,
            pltpu.roll(own, LANES - 1, 1) + pltpu.roll(ghost, 1, 1),
            pltpu.roll(own, 1, 1) + pltpu.roll(ghost, LANES - 1, 1),
        )
        later = (keep * ghost + rate * ((up + down) + side)) * has_side
        first = rate * ghost
        first_up = jnp.where(lanes < 4, 0.0, pltpu.roll(first, 4, 1))
        first_down = jnp.where(lanes >= LANES - 4, 0.0, pltpu.roll(first, LANES - 4, 1))
        outer = keep * first + rate * ((first_up + first_down) + later)
        second = rate * first
        terms = jnp.where(
            column < 2,
            jnp.where(column == 0, pltpu.roll(second, LANES - 2, 1), pltpu.roll(outer, LANES - 1, 1)),
            jnp.where(column == 2, pltpu.roll(outer, 1, 1), pltpu.roll(second, 2, 1)),
        )
        values = []
        for row in range(tiles):
            value = inner_ref[row, span, :] + jnp.where(
                near_edge, pltpu.roll(terms, (-(4 * row + 2)) % LANES, 1), 0.0
            )
            if row in row_terms:
                value = value + row_terms[row]
            values.append(value)
        out_ref[span, :, :] = jnp.swapaxes(jnp.stack(values, axis=0), 0, 1)

    for number in range(SPECIES // 8):
        slab(number)


def add_borders(inner, rows, near_row, far_row, near, far, own, rate):
    tiles = inner.shape[0]
    message = pl.BlockSpec((3, SR, LANES), lambda g: (0, 0, 0))
    edge = pl.BlockSpec((SPECIES, LANES), lambda g: (g, 0))
    flags = pl.BlockSpec((8, LANES), lambda g: (SR // 8 - 1, 0))
    return pl.pallas_call(
        functools.partial(border_kernel, tiles),
        grid=(SR // SPECIES,),
        in_specs=[
            pl.BlockSpec((tiles, SPECIES, LANES), lambda g: (0, g, 0)),
            pl.BlockSpec((1, SPECIES, LANES), lambda g: (0, g, 0)),
            pl.BlockSpec((1, SPECIES, LANES), lambda g: (3, g, 0)),
            message,
            message,
            edge,
            edge,
            flags,
            flags,
            edge,
            edge,
        ],
        out_specs=pl.BlockSpec((SPECIES, tiles, LANES), lambda g: (g, 0, 0)),
        out_shape=jax.ShapeDtypeStruct((S, tiles, LANES), jnp.float32),
        compiler_params=pltpu.CompilerParams(vmem_limit_bytes=TIGHT_VMEM),
        name="add_borders",
    )(inner, rows, rows, near_row, far_row, near, far, near, far, own, rate)


def trade(near_value, far_value, axis):
    count = lax.axis_size(axis)
    near = [(i, i ^ 1) for i in range(count) if i ^ 1 < count]
    far = [(i, j) for i in range(count) for j in [i + 1 if i % 2 else i - 1] if 0 <= j < count]
    return lax.ppermute(near_value, axis, near), lax.ppermute(far_value, axis, far)


def on_device(species_state, stiffness, send_list, jacobian, pattern, diffusivity):
    boxes = lax.axis_size("box")
    tiles = species_state.shape[0]
    slots = jacobian.shape[0] // boxes
    by_box = jacobian.reshape(boxes, slots, SP, SP)
    counts = stiffness.reshape(1, tiles)
    table = send_list.transpose(0, 1, 3, 2).reshape(slots, boxes)
    by_block = pattern.transpose(1, 2, 3, 0).reshape(NB, NB, boxes * slots)
    plan, rate, state, first, second = pack_all(
        by_box, by_block, table, counts, diffusivity.reshape(1, S), species_state.transpose(1, 0, 2)
    )
    plan, rate, state, first, second = lax.optimization_barrier(
        (plan, rate, state, first, second)
    )

    def exchange(packed):
        arrived = lax.all_to_all(packed, "box", split_axis=0, concat_axis=0, tiled=True)
        return arrived.reshape(-1, PACK, LANES)

    first = exchange(first)
    plan, rate, state, first, second = lax.optimization_barrier(
        (plan, rate, state, first, second)
    )
    second = exchange(second)
    early, rows, edge = solve_chunk(0, plan, state, (first, second), None, None, None)
    reacted, rows, edge = solve_chunk(1, plan, state, (first, second), early, rows, edge)

    near, far = trade(edge, edge, "bal")
    near_row, far_row = trade(*make_messages(rows, near, far), "box")
    inner = diffuse_inside(reacted, rate)
    field = add_borders(inner, rows, near_row, far_row, near, far, edge, rate)
    return field.transpose(1, 0, 2)


def solution(mesh):
    in_specs = (
        P("box", None, "bal"),
        P("box", "bal"),
        P("box", "bal", None, None),
        P("box", "bal", None, None),
        P("box", "bal", None, None),
        P(),
    )
    return jax.shard_map(
        on_device,
        mesh=mesh,
        in_specs=in_specs,
        out_specs=P("box", None, "bal"),
        check_vma=False,
    )
```

```python
import functools

import jax
import numpy as np
import jax.numpy as jnp
from jax import lax
from jax.experimental import pallas as pl
from jax.experimental.pallas import tpu as pltpu
from jax.sharding import PartitionSpec as P

S = 218
SR = 224
SP = 256
BL = 64
NB = 4
PACK = 400
LANES = 128
EPSILON = 1e-06
GROUP = 8
SLOTS = 4
CHUNKS = ((0, 3), (3, 1))
PACK_BOXES = 8
TURN_SPECIES = 112
SPECIES = 56
WIDE_VMEM = 63 * 1024 * 1024
INNER_VMEM = 48 * 1024 * 1024
TIGHT_VMEM = 40 * 1024 * 1024


def lane_iota(rows):
    return lax.broadcasted_iota(jnp.int32, (rows, LANES), 1)


def make_plan(table, counts):
    slots, boxes = table.shape
    tiles = counts.shape[1]
    size = float(LANES)
    filler = jnp.full((slots, LANES - boxes), -1.0, jnp.float32)
    spread = jnp.concatenate([table.astype(jnp.float32), filler], axis=1)
    counts = jnp.concatenate(
        [counts.astype(jnp.float32), jnp.zeros((1, LANES - tiles), jnp.float32)], axis=1
    )
    lane = lane_iota(LANES).astype(jnp.float32)
    item = lax.broadcasted_iota(jnp.int32, (LANES, LANES), 0).astype(jnp.float32)
    row = jnp.full((1, LANES), -1.0, jnp.float32)
    for slot in range(slots):
        part = pltpu.roll(spread, slot * boxes, 1)[slot : slot + 1] if slot else spread[0:1]
        here = (lane_iota(1) >= slot * boxes) & (lane_iota(1) < (slot + 1) * boxes)
        row = jnp.where(here, part, row)
    tile = jnp.transpose(jnp.broadcast_to(row, (LANES, LANES)))
    turns = jnp.sum(jnp.where(tile == lane, counts, 0.0), axis=1, keepdims=True)
    turns = jnp.broadcast_to(turns, (LANES, LANES))
    live = tile >= 0.0
    early_size = CHUNKS[0][1] * boxes
    early = live & (item < early_size)
    weight = (size - turns) * size + item

    def rank(key):
        smaller = jnp.where(jnp.transpose(key) < key, 1.0, 0.0)
        return jnp.broadcast_to(jnp.sum(smaller, axis=1, keepdims=True), (LANES, LANES))

    late = 4.0 * size * size
    begun = jnp.sum(jnp.where(early, 1.0, 0.0), axis=0, keepdims=True)
    begun = jnp.floor(begun * (1.0 / GROUP)) * GROUP
    chosen = early & (rank(jnp.where(early, weight, late + item)) < begun)
    place = rank(weight + jnp.where(chosen, 0.0, jnp.where(live, late, 2.0 * late)))
    slot_of = jnp.floor(item * (1.0 / boxes))
    box_of = item - slot_of * boxes
    width = float(CHUNKS[0][1])
    source = jnp.where(item < early_size, box_of * width + slot_of, item)
    rows = [
        jnp.sum(jnp.where(place == lane, value, 0.0), axis=0, keepdims=True)
        for value in (source, tile, turns)
    ]
    rows += [begun, jnp.zeros((4, LANES), jnp.float32)]
    return jnp.concatenate(rows, axis=0).astype(jnp.int32)


def pack_kernel(pattern_ref, table_ref, counts_ref, diffusivity_ref, cells_ref, jac_ref,
                plan_ref, rate_ref, state_ref, *out_refs):
    @pl.when(pl.program_id(0) == 0)
    def _():
        plan_ref[...] = make_plan(table_ref[...], counts_ref[...])
        row = jnp.concatenate(
            [diffusivity_ref[...], jnp.zeros((1, SP - S), jnp.float32)], axis=1
        )
        for start in (0, LANES):
            rows = min(LANES, SR - start)
            part = jnp.broadcast_to(row[:, start : start + LANES], (LANES, LANES))
            rate_ref[start : start + rows, :] = jnp.transpose(part)[0:rows]

    state_ref[...] = cells_ref[...].astype(jnp.float32)

    low_half = lane_iota(1) < BL
    half_rows = SR // 2
    tail = SR - (NB - 1) * BL
    inside = lax.broadcasted_iota(jnp.int32, (tail, LANES), 0) < S - (NB - 1) * BL
    inside = inside.astype(jnp.float32).astype(jnp.bfloat16)
    middle_lane = lane_iota(half_rows)
    edge_lane = lane_iota(BL)

    def one_box(inner, carry):
        box = pl.program_id(0) * PACK_BOXES + inner
        for slot in range(SLOTS):
            chunk = next(k for k, (at, n) in enumerate(CHUNKS) if at <= slot < at + n)
            put = functools.partial(out_refs[chunk].__setitem__)
            place = slot - CHUNKS[chunk][0]
            held = box * SLOTS + slot
            right = []
            for p in range(NB):
                rows = min(SR, (p + 1) * BL) - p * BL
                parts = []
                for half in range(2):
                    mask = jnp.where(
                        low_half,
                        pattern_ref[p, 2 * half, held].astype(jnp.float32),
                        pattern_ref[p, 2 * half + 1, held].astype(jnp.float32),
                    ).astype(jnp.bfloat16)
                    value = (
                        jac_ref[inner, slot, p * BL : p * BL + rows, half * LANES : (half + 1) * LANES]
                        * mask
                    )
                    parts.append(value * inside if p == NB - 1 else value)
                put((inner, place, slice(p * BL, p * BL + rows), slice(None)), parts[0])
                right.append(parts[1])
            upper = jnp.concatenate([right[0], right[1][: half_rows - BL]], axis=0)
            lower = jnp.concatenate([right[1][half_rows - BL :], right[2], right[3]], axis=0)
            middle = jnp.where(middle_lane < BL, upper, pltpu.roll(lower, BL, 1))
            put((inner, place, slice(SR, SR + half_rows), slice(None)), middle)
            last = jnp.concatenate([right[3], jnp.zeros((BL - tail, LANES), jnp.bfloat16)], axis=0)
            edge = jnp.where(
                edge_lane < 64,
                jnp.where(edge_lane < 32, pltpu.roll(right[0], 64, 1), pltpu.roll(right[1], 96, 1)),
                jnp.where(edge_lane < 96, right[2], pltpu.roll(last, 32, 1)),
            )
            put((inner, place, slice(SR + half_rows, PACK), slice(None)), edge)
        return carry

    lax.fori_loop(0, PACK_BOXES, one_box, 0, unroll=4)


def pack_all(jacobian, pattern, table, counts, diffusivity, cells):
    boxes = jacobian.shape[0]
    tiles = cells.shape[1]
    last = (S - 1) // TURN_SPECIES
    return pl.pallas_call(
        pack_kernel,
        grid=(boxes // PACK_BOXES,),
        in_specs=[
            pl.BlockSpec(memory_space=pltpu.SMEM),
            pl.BlockSpec(table.shape, lambda b: (0, 0)),
            pl.BlockSpec(counts.shape, lambda b: (0, 0)),
            pl.BlockSpec(diffusivity.shape, lambda b: (0, 0)),
            pl.BlockSpec(
                (TURN_SPECIES, tiles, LANES), lambda b: (jnp.minimum(b, last), 0, 0)
            ),
            pl.BlockSpec((PACK_BOXES, SLOTS, SR, SP), lambda b: (b, 0, 0, 0)),
        ],
        out_specs=[
            pl.BlockSpec((8, LANES), lambda b: (0, 0)),
            pl.BlockSpec((SR, LANES), lambda b: (0, 0)),
            pl.BlockSpec(
                (TURN_SPECIES, tiles, LANES), lambda b: (jnp.minimum(b, last), 0, 0)
            ),
        ]
        + [
            pl.BlockSpec((PACK_BOXES, n, PACK, LANES), lambda b: (b, 0, 0, 0)) for _, n in CHUNKS
        ],
        out_shape=[
            jax.ShapeDtypeStruct((8, LANES), jnp.int32),
            jax.ShapeDtypeStruct((SR, LANES), jnp.float32),
            jax.ShapeDtypeStruct((S, tiles, LANES), jnp.float32),
        ]
        + [
            jax.ShapeDtypeStruct((boxes, n, PACK, LANES), jnp.bfloat16) for _, n in CHUNKS
        ],
        compiler_params=pltpu.CompilerParams(vmem_limit_bytes=WIDE_VMEM),
        name="pack_all",
    )(pattern, table, counts, diffusivity, cells, jacobian)


def unpack(packed_ref, item, dense_ref):
    half_rows = SR // 2
    dense_ref[:, 0:LANES] = packed_ref[item, pl.ds(0, SR), :]
    middle = packed_ref[item, pl.ds(SR, half_rows), :]
    edge = packed_ref[item, pl.ds(SR + half_rows, BL), :]
    high = pltpu.roll(middle, BL, 1)

    def put(row, rows, low, rest):
        dense_ref[pl.ds(row, rows), LANES:SP] = jnp.where(lane_iota(rows) < BL, low, rest)

    put(0, 64, middle[0:64], pltpu.roll(edge, 64, 1))
    shifted = pltpu.roll(edge, 32, 1)
    put(64, 48, middle[64:112], shifted[0:48])
    put(112, 16, high[0:16], shifted[48:64])
    put(128, 64, high[16:80], edge)
    put(192, 32, high[80:112], pltpu.roll(edge[0:32], 96, 1))


def solve_kernel(chunk, *refs):
    if chunk == 0:
        plan_ref, state_hbm, packed_hbm, out_hbm, rows_hbm, edge_ref = refs[:6]
        scratch = refs[6:]
    else:
        plan_ref, state_hbm, packed_hbm, second_hbm, _, _, edge_in = refs[:7]
        out_hbm, rows_hbm, edge_ref = refs[7:10]
        scratch = refs[10:]
    packed, state, outgoing, arrived, sent = scratch[:5]
    dense, right, left_over, mapped, guess, sums = (
        scratch[5 + GROUP * kind : 5 + GROUP * (kind + 1)] for kind in range(6)
    )
    tiles = state_hbm.shape[1]
    begun = plan_ref[3, 0]
    base = 0 if chunk == 0 else begun
    groups = (begun if chunk == 0 else tiles - begun) // GROUP

    def fetch(place, origin, at):
        return pltpu.make_async_copy(origin.at[at], packed.at[place], arrived.at[0, place])

    def fetch_state(place):
        tile = plan_ref[1, base + place]
        return pltpu.make_async_copy(
            state_hbm.at[:, tile, :], state.at[place, 0:S], arrived.at[1, place]
        )

    def start_fetch(place, carry):
        at = plan_ref[0, base + place]
        state[place, SR - 8 : SR, :] = jnp.zeros((8, LANES), jnp.float32)
        fetch_state(place).start()
        if chunk == 0:
            fetch(place, packed_hbm, at).start()
        else:
            early = packed_hbm.shape[0]

            @pl.when(at < early)
            def _():
                fetch(place, packed_hbm, at).start()

            @pl.when(at >= early)
            def _():
                fetch(place, second_hbm, at - early).start()

        return carry

    lax.fori_loop(0, groups * GROUP, start_fetch, 0)
    for member in range(GROUP):
        right[member][SR:SP, :] = jnp.zeros((SP - SR, SP), jnp.bfloat16)
    if chunk == 0:
        edge_ref[...] = jnp.zeros_like(edge_ref)
    else:
        edge_ref[...] = edge_in[...]
    edge_lane = lane_iota(SR) // 4

    def send(buffer, member, tile):
        return pltpu.make_async_copy(
            outgoing.at[buffer, member], out_hbm.at[tile], sent.at[buffer, member]
        )

    def send_row(buffer, member, tile):
        at = jnp.where(tile < 2, tile, tile - (tiles - 4))
        return pltpu.make_async_copy(
            outgoing.at[buffer, member], rows_hbm.at[at], sent.at[2 + buffer, member]
        )

    def is_row(tile):
        return (tile < 2) | (tile >= tiles - 2)

    def drain(group_no):
        for member in range(GROUP):
            tile = plan_ref[1, base + group_no * GROUP + member]
            send(group_no % 2, member, tile).wait()

            @pl.when(is_row(tile))
            def _():
                send_row(group_no % 2, member, tile).wait()

    def split(member, row, rows, remainder):
        high = remainder.astype(jnp.bfloat16)
        span = slice(row, row + rows)
        right[member][span, 0:LANES] = high
        right[member][span, LANES:SP] = (remainder - high.astype(jnp.float32)).astype(
            jnp.bfloat16
        )

    def multiply(member):
        return jnp.dot(
            dense[member][...], right[member][...], preferred_element_type=jnp.float32
        )

    def measure(member, product):
        above = jnp.zeros((8, LANES), jnp.float32)
        below = jnp.zeros((8, LANES), jnp.float32)
        for row in range(0, SR, 8):
            span = slice(row, row + 8)
            remainder = left_over[member][span, :]
            value = remainder - (product[span, 0:LANES] + product[span, LANES:SP])
            mapped[member][span, :] = value
            above = above + remainder * value
            below = below + value * value
        return above, below

    def move(member, above, below, active):
        above = jnp.sum(above, axis=0, keepdims=True)
        below = jnp.sum(below, axis=0, keepdims=True) + EPSILON
        step = jnp.where(active, above / below, 0.0)
        for row in range(0, SR, 16):
            span = slice(row, row + 16)
            remainder = left_over[member][span, :]
            guess[member][span, :] += step * remainder
            remainder = remainder - step * mapped[member][span, :]
            left_over[member][span, :] = remainder
            split(member, row, 16, remainder)

    def keep_sums(member, above, below):
        sums[member][0:8, :] = above
        sums[member][8:16, :] = below

    def one_group(group_no, carry):
        buffer = group_no % 2
        places = [group_no * GROUP + member for member in range(GROUP)]
        chosen = [plan_ref[1, base + place] for place in places]
        counts = [plan_ref[2, base + place] for place in places]

        for member in range(GROUP):
            fetch(places[member], packed_hbm, 0).wait()
            fetch_state(places[member]).wait()
        for member in range(GROUP):
            unpack(packed, places[member], dense[member])
            start_value = state[places[member]]
            right[member][0:SR, 0:LANES] = start_value.astype(jnp.bfloat16)
            guess[member][...] = start_value
        for member in range(GROUP):
            remainder = jnp.dot(
                dense[member][...],
                right[member][:, 0:LANES],
                preferred_element_type=jnp.float32,
            )
            left_over[member][...] = remainder
            split(member, 0, SR, remainder)

        half = GROUP // 2
        for member in range(half, GROUP):
            keep_sums(member, *measure(member, multiply(member)))

        def advance(turn_no, inner):
            for one, other in zip(range(half), range(half, GROUP)):
                product = multiply(one)
                move(other, sums[other][0:8, :], sums[other][8:16, :], turn_no < counts[other])
                next_product = multiply(other)
                move(one, *measure(one, product), turn_no < counts[one])
                keep_sums(other, *measure(other, next_product))
            return inner

        lax.fori_loop(0, functools.reduce(jnp.maximum, counts), advance, 0)

        @pl.when(group_no >= 2)
        def _():
            drain(group_no - 2)

        for member in range(GROUP):
            result = guess[member][...]
            outgoing[buffer, member] = result
            tile = chosen[member]
            edge_ref[...] = jnp.where(
                edge_lane == tile, pltpu.roll(result, (4 * tile + 2) % LANES, 1), edge_ref[...]
            )
            send(buffer, member, tile).start()

            @pl.when(is_row(tile))
            def _():
                send_row(buffer, member, tile).start()

        return carry

    lax.fori_loop(0, groups, one_group, 0)

    for back in range(2):
        @pl.when(groups > back)
        def _():
            drain(groups - 1 - back)

    edge_ref[S + 2 : SR, :] = jnp.ones((SR - S - 2, LANES), jnp.float32)


def solve_chunk(chunk, plan, state, packed, reacted, rows, edge):
    tiles = state.shape[1]
    out_shape = (
        jax.ShapeDtypeStruct((tiles, SR, LANES), jnp.float32),
        jax.ShapeDtypeStruct((4, SR, LANES), jnp.float32),
        jax.ShapeDtypeStruct((SR, LANES), jnp.float32),
    )
    anywhere = pl.BlockSpec(memory_space=pl.ANY)
    vmem = pl.BlockSpec(memory_space=pltpu.VMEM)
    in_specs = [pl.BlockSpec(memory_space=pltpu.SMEM), anywhere]
    in_specs += [anywhere] * (chunk + 1)
    operands = [plan, state, *packed[: chunk + 1]]
    aliases = {}
    if chunk:
        in_specs += [anywhere, anywhere, vmem]
        operands += [reacted, rows, edge]
        aliases = {4: 0, 5: 1}
    tile_values = pltpu.VMEM((SR, LANES), jnp.float32)
    return pl.pallas_call(
        functools.partial(solve_kernel, chunk),
        in_specs=in_specs,
        out_specs=(anywhere, anywhere, vmem),
        out_shape=out_shape,
        input_output_aliases=aliases,
        scratch_shapes=[
            pltpu.VMEM((tiles, PACK, LANES), jnp.bfloat16),
            pltpu.VMEM((tiles, SR, LANES), jnp.float32),
            pltpu.VMEM((2, GROUP, SR, LANES), jnp.float32),
            pltpu.SemaphoreType.DMA((2, tiles)),
            pltpu.SemaphoreType.DMA((4, GROUP)),
        ]
        + [pltpu.VMEM((SR, SP), jnp.bfloat16)] * GROUP
        + [pltpu.VMEM((SP, SP), jnp.bfloat16)] * GROUP
        + [tile_values] * (3 * GROUP)
        + [pltpu.VMEM((16, LANES), jnp.float32)] * GROUP,
        compiler_params=pltpu.CompilerParams(vmem_limit_bytes=WIDE_VMEM),
        cost_estimate=pl.CostEstimate(
            flops=16 * 300_000_000, bytes_accessed=16 * 200000, transcendentals=0
        ),
        name="solve_chunk",
    )(*operands)


def is_odd(axis):
    return lax.rem(lax.axis_index(axis), 2) == 1


def message_kernel(rows_ref, near_ref, far_ref, near_out_ref, far_out_ref):
    tiles = LANES // 4
    lanes = lane_iota(SR)
    odd = is_odd("bal")
    low = jnp.where(odd, near_ref[...], far_ref[...])
    high = jnp.where(odd, far_ref[...], near_ref[...])
    odd = is_odd("box")

    def message(start, row, near):
        for to_near, out_ref in ((near, near_out_ref), (jnp.logical_not(near), far_out_ref)):

            @pl.when(to_near)
            def _():
                out_ref[0:2] = rows_ref[start : start + 2]
                cells = jnp.where(
                    lanes == 0,
                    pltpu.roll(low, (-(4 * row + 1)) % LANES, 1),
                    pltpu.roll(high, (-(4 * row + 3)) % LANES, 1),
                )
                out_ref[2] = jnp.where(lanes == 2, 1.0, cells).astype(jnp.bfloat16)

    message(0, 0, odd)
    message(2, tiles - 1, jnp.logical_not(odd))


def make_messages(rows, near, far):
    vmem = pl.BlockSpec(memory_space=pltpu.VMEM)
    shape = jax.ShapeDtypeStruct((3, SR, LANES), jnp.bfloat16)
    return pl.pallas_call(
        message_kernel,
        in_specs=[vmem, vmem, vmem],
        out_specs=(vmem, vmem),
        out_shape=(shape, shape),
        compiler_params=pltpu.CompilerParams(vmem_limit_bytes=TIGHT_VMEM),
        name="make_messages",
    )(rows, near, far)


def beside(value, lanes):
    return jnp.where(lanes == 0, 0.0, pltpu.roll(value, 1, 1)) + jnp.where(
        lanes == LANES - 1, 0.0, pltpu.roll(value, LANES - 1, 1)
    )


def inner_kernel(tiles, block_hbm, rate_ref, both_ref, out_ref, block_ref, arrived):
    zero = jnp.zeros((1, 8, LANES), jnp.float32)
    copies = [
        pltpu.make_async_copy(
            block_hbm.at[:, at : at + SPECIES, :], block_ref.at[:, at : at + SPECIES, :], arrived.at[k]
        )
        for k, at in enumerate(range(0, SR, SPECIES))
    ]
    for copy in copies:
        copy.start()

    def around(value, by):
        gap = jnp.concatenate([zero] * by, axis=0)
        return jnp.concatenate([gap, value[: tiles - by]], axis=0) + jnp.concatenate(
            [value[by:], gap], axis=0
        )

    for number in range(SR // 8):
        if number * 8 % SPECIES == 0:
            copies[number * 8 // SPECIES].wait()
        span = slice(number * 8, number * 8 + 8)
        rate = rate_ref[span, :]
        keep = 1.0 - 4.0 * rate
        square = rate * rate
        cells = block_ref[:, span, :]
        flat = cells.reshape(tiles * 8, LANES)
        high = flat.astype(jnp.bfloat16)
        low = (flat - high.astype(jnp.float32)).astype(jnp.bfloat16)
        product = jnp.dot(
            jnp.concatenate([high, low], axis=1), both_ref[...], preferred_element_type=jnp.float32
        )
        once = product[:, 0:LANES].reshape(tiles, 8, LANES)
        twice = product[:, LANES:].reshape(tiles, 8, LANES)
        near = (2.0 * keep * rate) * (around(cells, 1) + once)
        sides = around(once, 1)
        far = square * ((around(cells, 2) + twice) + (sides + sides))
        own = keep * keep + 2.0 * square
        end = keep * keep + square
        value = near + far
        out_ref[1 : tiles - 1, span, :] = value[1 : tiles - 1] + own * cells[1 : tiles - 1]
        out_ref[0, span, :] = value[0] + end * cells[0]
        out_ref[tiles - 1, span, :] = value[tiles - 1] + end * cells[tiles - 1]


def diffuse_inside(block, rate):
    tiles = block.shape[0]
    vmem = pl.BlockSpec(memory_space=pltpu.VMEM)
    place = np.arange(LANES)
    next_to = (np.abs(place[:, None] - place[None, :]) == 1).astype(np.float32)
    both = np.concatenate([next_to, next_to @ next_to], axis=1)
    both = jnp.asarray(np.concatenate([both, both], axis=0), jnp.bfloat16)
    return pl.pallas_call(
        functools.partial(inner_kernel, tiles),
        in_specs=[pl.BlockSpec(memory_space=pl.ANY), vmem, vmem],
        out_specs=vmem,
        out_shape=jax.ShapeDtypeStruct(block.shape, jnp.float32),
        scratch_shapes=[
            pltpu.VMEM(block.shape, jnp.float32),
            pltpu.SemaphoreType.DMA((SR // SPECIES,)),
        ],
        compiler_params=pltpu.CompilerParams(vmem_limit_bytes=INNER_VMEM),
        cost_estimate=pl.CostEstimate(
            flops=tiles * SR * LANES * 20, bytes_accessed=8 * block.size, transcendentals=0
        ),
        name="diffuse_inside",
    )(block, rate, both)


def border_kernel(tiles, inner_ref, top_ref, bottom_ref, near_row_ref, far_row_ref, near_ref,
                  far_ref, near_here_ref, far_here_ref, own_ref, rate_ref, out_ref):
    lanes = lane_iota(8)
    column = lanes % 4
    here = S + 2 - (SR - 8)
    from_near = (column < 2) == is_odd("bal")
    near_above = is_odd("box")
    has_side = jnp.where(
        from_near, near_here_ref[here : here + 1, :], far_here_ref[here : here + 1, :]
    )
    near_edge = (lanes < 2) | (lanes >= LANES - 2)

    def slab(number):
        span = slice(number * 8, number * 8 + 8)
        overall = pl.program_id(0) * (SPECIES // 8) + number
        wide = pl.ds(pl.multiple_of(overall // 2 * 16, 16), 16)

        def read(ref, row):
            both = ref[row, wide, :].astype(jnp.float32)
            return jnp.where(overall % 2 == 0, both[0:8], both[8:16])

        near_rows = [read(near_row_ref, row) for row in range(3)]
        far_rows = [read(far_row_ref, row) for row in range(3)]
        above = [jnp.where(near_above, a, b) for a, b in zip(near_rows, far_rows)]
        below = [jnp.where(near_above, b, a) for a, b in zip(near_rows, far_rows)]

        rate = rate_ref[span, :]
        keep = 1.0 - 4.0 * rate
        own = own_ref[span, :]
        ghost = jnp.where(from_near, near_ref[span, :], far_ref[span, :])

        def rows_beside(near, far, inner, corner):
            exists = jnp.broadcast_to(corner[:, 2:3], (8, LANES))
            left = jnp.where(lanes == 0, corner, pltpu.roll(near, 1, 1))
            right = jnp.where(lanes == LANES - 1, corner, pltpu.roll(near, LANES - 1, 1))
            later = (keep * near + rate * ((far + inner) + (left + right))) * exists
            first = rate * near
            outer = keep * first + rate * (beside(first, lanes) + later)
            return outer, rate * first

        corner_above, corner_below = above[2], below[2]
        row_terms = {}
        row_terms[0], row_terms[1] = rows_beside(
            above[1], above[0], top_ref[0, span, :], corner_above
        )
        row_terms[tiles - 1], row_terms[tiles - 2] = rows_beside(
            below[0], below[1], bottom_ref[0, span, :], corner_below
        )

        up = pltpu.roll(ghost, 4, 1)
        up = jnp.where(lanes == 1, pltpu.roll(corner_above, 1, 1), up)
        up = jnp.where(lanes == 2, pltpu.roll(corner_above, 3, 1), up)
        down = pltpu.roll(ghost, LANES - 4, 1)
        down = jnp.where(lanes == LANES - 3, pltpu.roll(corner_below, LANES - 3, 1), down)
        down = jnp.where(lanes == LANES - 2, pltpu.roll(corner_below, LANES - 1, 1), down)
        side = jnp.where(
            column == 1,
            pltpu.roll(own, LANES - 1, 1) + pltpu.roll(ghost, 1, 1),
            pltpu.roll(own, 1, 1) + pltpu.roll(ghost, LANES - 1, 1),
        )
        later = (keep * ghost + rate * ((up + down) + side)) * has_side
        first = rate * ghost
        first_up = jnp.where(lanes < 4, 0.0, pltpu.roll(first, 4, 1))
        first_down = jnp.where(lanes >= LANES - 4, 0.0, pltpu.roll(first, LANES - 4, 1))
        outer = keep * first + rate * ((first_up + first_down) + later)
        second = rate * first
        terms = jnp.where(
            column < 2,
            jnp.where(column == 0, pltpu.roll(second, LANES - 2, 1), pltpu.roll(outer, LANES - 1, 1)),
            jnp.where(column == 2, pltpu.roll(outer, 1, 1), pltpu.roll(second, 2, 1)),
        )
        values = []
        for row in range(tiles):
            value = inner_ref[row, span, :] + jnp.where(
                near_edge, pltpu.roll(terms, (-(4 * row + 2)) % LANES, 1), 0.0
            )
            if row in row_terms:
                value = value + row_terms[row]
            values.append(value)
        out_ref[span, :, :] = jnp.swapaxes(jnp.stack(values, axis=0), 0, 1)

    for number in range(SPECIES // 8):
        slab(number)


def add_borders(inner, rows, near_row, far_row, near, far, own, rate):
    tiles = inner.shape[0]
    message = pl.BlockSpec((3, SR, LANES), lambda g: (0, 0, 0))
    edge = pl.BlockSpec((SPECIES, LANES), lambda g: (g, 0))
    flags = pl.BlockSpec((8, LANES), lambda g: (SR // 8 - 1, 0))
    return pl.pallas_call(
        functools.partial(border_kernel, tiles),
        grid=(SR // SPECIES,),
        in_specs=[
            pl.BlockSpec((tiles, SPECIES, LANES), lambda g: (0, g, 0)),
            pl.BlockSpec((1, SPECIES, LANES), lambda g: (0, g, 0)),
            pl.BlockSpec((1, SPECIES, LANES), lambda g: (3, g, 0)),
            message,
            message,
            edge,
            edge,
            flags,
            flags,
            edge,
            edge,
        ],
        out_specs=pl.BlockSpec((SPECIES, tiles, LANES), lambda g: (g, 0, 0)),
        out_shape=jax.ShapeDtypeStruct((S, tiles, LANES), jnp.float32),
        compiler_params=pltpu.CompilerParams(vmem_limit_bytes=TIGHT_VMEM),
        name="add_borders",
    )(inner, rows, rows, near_row, far_row, near, far, near, far, own, rate)


def trade(near_value, far_value, axis):
    count = lax.axis_size(axis)
    near = [(i, i ^ 1) for i in range(count) if i ^ 1 < count]
    far = [(i, j) for i in range(count) for j in [i + 1 if i % 2 else i - 1] if 0 <= j < count]
    return lax.ppermute(near_value, axis, near), lax.ppermute(far_value, axis, far)


def on_device(species_state, stiffness, send_list, jacobian, pattern, diffusivity):
    boxes = lax.axis_size("box")
    tiles = species_state.shape[0]
    slots = jacobian.shape[0] // boxes
    by_box = jacobian.reshape(boxes, slots, SP, SP)
    counts = stiffness.reshape(1, tiles)
    table = send_list.transpose(0, 1, 3, 2).reshape(slots, boxes)
    by_block = pattern.transpose(1, 2, 3, 0).reshape(NB, NB, boxes * slots)
    plan, rate, state, first, second = pack_all(
        by_box, by_block, table, counts, diffusivity.reshape(1, S), species_state.transpose(1, 0, 2)
    )
    plan, rate, state, first, second = lax.optimization_barrier(
        (plan, rate, state, first, second)
    )

    def exchange(packed):
        arrived = lax.all_to_all(packed, "box", split_axis=0, concat_axis=0, tiled=True)
        return arrived.reshape(-1, PACK, LANES)

    first = exchange(first)
    plan, rate, state, first, second = lax.optimization_barrier(
        (plan, rate, state, first, second)
    )
    second = exchange(second)
    early, rows, edge = solve_chunk(0, plan, state, (first, second), None, None, None)
    reacted, rows, edge = solve_chunk(1, plan, state, (first, second), early, rows, edge)

    near, far = trade(edge, edge, "bal")
    messages = make_messages(rows.astype(jnp.bfloat16), near, far)
    near_row, far_row = trade(*messages, "box")
    inner = diffuse_inside(reacted, rate)
    field = add_borders(inner, rows, near_row, far_row, near, far, edge, rate)
    return field.transpose(1, 0, 2)


def solution(mesh):
    in_specs = (
        P("box", None, "bal"),
        P("box", "bal"),
        P("box", "bal", None, None),
        P("box", "bal", None, None),
        P("box", "bal", None, None),
        P(),
    )
    return jax.shard_map(
        on_device,
        mesh=mesh,
        in_specs=in_specs,
        out_specs=P("box", None, "bal"),
        check_vma=False,
    )
```

```python
import functools

import jax
import numpy as np
import jax.numpy as jnp
from jax import lax
from jax.experimental import pallas as pl
from jax.experimental.pallas import tpu as pltpu
from jax.sharding import PartitionSpec as P

S = 218
SR = 224
SP = 256
BL = 64
NB = 4
PACK = 400
LANES = 128
EPSILON = 1e-06
GROUP = 8
SLOTS = 4
CHUNKS = ((0, 3), (3, 1))
PACK_BOXES = 8
TURN_SPECIES = 112
SPECIES = 56
WIDE_VMEM = 63 * 1024 * 1024
INNER_VMEM = 48 * 1024 * 1024
TIGHT_VMEM = 40 * 1024 * 1024


def lane_iota(rows):
    return lax.broadcasted_iota(jnp.int32, (rows, LANES), 1)


def make_plan(table, counts):
    slots, boxes = table.shape
    tiles = counts.shape[1]
    size = float(LANES)
    filler = jnp.full((slots, LANES - boxes), -1.0, jnp.float32)
    spread = jnp.concatenate([table.astype(jnp.float32), filler], axis=1)
    counts = jnp.concatenate(
        [counts.astype(jnp.float32), jnp.zeros((1, LANES - tiles), jnp.float32)], axis=1
    )
    lane = lane_iota(LANES).astype(jnp.float32)
    item = lax.broadcasted_iota(jnp.int32, (LANES, LANES), 0).astype(jnp.float32)
    row = jnp.full((1, LANES), -1.0, jnp.float32)
    for slot in range(slots):
        part = pltpu.roll(spread, slot * boxes, 1)[slot : slot + 1] if slot else spread[0:1]
        here = (lane_iota(1) >= slot * boxes) & (lane_iota(1) < (slot + 1) * boxes)
        row = jnp.where(here, part, row)
    tile = jnp.transpose(jnp.broadcast_to(row, (LANES, LANES)))
    turns = jnp.sum(jnp.where(tile == lane, counts, 0.0), axis=1, keepdims=True)
    turns = jnp.broadcast_to(turns, (LANES, LANES))
    live = tile >= 0.0
    early_size = CHUNKS[0][1] * boxes
    early = live & (item < early_size)
    weight = (size - turns) * size + item

    def rank(key):
        smaller = jnp.where(jnp.transpose(key) < key, 1.0, 0.0)
        return jnp.broadcast_to(jnp.sum(smaller, axis=1, keepdims=True), (LANES, LANES))

    late = 4.0 * size * size
    begun = jnp.sum(jnp.where(early, 1.0, 0.0), axis=0, keepdims=True)
    begun = jnp.floor(begun * (1.0 / GROUP)) * GROUP
    chosen = early & (rank(jnp.where(early, weight, late + item)) < begun)
    place = rank(weight + jnp.where(chosen, 0.0, jnp.where(live, late, 2.0 * late)))
    slot_of = jnp.floor(item * (1.0 / boxes))
    box_of = item - slot_of * boxes
    width = float(CHUNKS[0][1])
    source = jnp.where(item < early_size, box_of * width + slot_of, item)
    rows = [
        jnp.sum(jnp.where(place == lane, value, 0.0), axis=0, keepdims=True)
        for value in (source, tile, turns)
    ]
    rows += [begun, jnp.zeros((4, LANES), jnp.float32)]
    return jnp.concatenate(rows, axis=0).astype(jnp.int32)


def pack_kernel(pattern_ref, table_ref, counts_ref, diffusivity_ref, cells_ref, jac_ref,
                plan_ref, rate_ref, state_ref, *out_refs):
    @pl.when(pl.program_id(0) == 0)
    def _():
        plan_ref[...] = make_plan(table_ref[...], counts_ref[...])
        row = jnp.concatenate(
            [diffusivity_ref[...], jnp.zeros((1, SP - S), jnp.float32)], axis=1
        )
        for start in (0, LANES):
            rows = min(LANES, SR - start)
            part = jnp.broadcast_to(row[:, start : start + LANES], (LANES, LANES))
            rate_ref[start : start + rows, :] = jnp.transpose(part)[0:rows]

    state_ref[...] = cells_ref[...].astype(jnp.float32)

    low_half = lane_iota(1) < BL
    half_rows = SR // 2
    tail = SR - (NB - 1) * BL
    inside = lax.broadcasted_iota(jnp.int32, (tail, LANES), 0) < S - (NB - 1) * BL
    inside = inside.astype(jnp.float32).astype(jnp.bfloat16)
    middle_lane = lane_iota(half_rows)
    edge_lane = lane_iota(BL)

    def one_box(inner, carry):
        box = pl.program_id(0) * PACK_BOXES + inner
        for slot in range(SLOTS):
            chunk = next(k for k, (at, n) in enumerate(CHUNKS) if at <= slot < at + n)
            put = functools.partial(out_refs[chunk].__setitem__)
            place = slot - CHUNKS[chunk][0]
            held = box * SLOTS + slot
            right = []
            for p in range(NB):
                rows = min(SR, (p + 1) * BL) - p * BL
                parts = []
                for half in range(2):
                    mask = jnp.where(
                        low_half,
                        pattern_ref[p, 2 * half, held].astype(jnp.float32),
                        pattern_ref[p, 2 * half + 1, held].astype(jnp.float32),
                    ).astype(jnp.bfloat16)
                    value = (
                        jac_ref[inner, slot, p * BL : p * BL + rows, half * LANES : (half + 1) * LANES]
                        * mask
                    )
                    parts.append(value * inside if p == NB - 1 else value)
                put((inner, place, slice(p * BL, p * BL + rows), slice(None)), parts[0])
                right.append(parts[1])
            upper = jnp.concatenate([right[0], right[1][: half_rows - BL]], axis=0)
            lower = jnp.concatenate([right[1][half_rows - BL :], right[2], right[3]], axis=0)
            middle = jnp.where(middle_lane < BL, upper, pltpu.roll(lower, BL, 1))
            put((inner, place, slice(SR, SR + half_rows), slice(None)), middle)
            last = jnp.concatenate([right[3], jnp.zeros((BL - tail, LANES), jnp.bfloat16)], axis=0)
            edge = jnp.where(
                edge_lane < 64,
                jnp.where(edge_lane < 32, pltpu.roll(right[0], 64, 1), pltpu.roll(right[1], 96, 1)),
                jnp.where(edge_lane < 96, right[2], pltpu.roll(last, 32, 1)),
            )
            put((inner, place, slice(SR + half_rows, PACK), slice(None)), edge)
        return carry

    lax.fori_loop(0, PACK_BOXES, one_box, 0, unroll=4)


def pack_all(jacobian, pattern, table, counts, diffusivity, cells):
    boxes = jacobian.shape[0]
    tiles = cells.shape[1]
    last = (S - 1) // TURN_SPECIES
    return pl.pallas_call(
        pack_kernel,
        grid=(boxes // PACK_BOXES,),
        in_specs=[
            pl.BlockSpec(memory_space=pltpu.SMEM),
            pl.BlockSpec(table.shape, lambda b: (0, 0)),
            pl.BlockSpec(counts.shape, lambda b: (0, 0)),
            pl.BlockSpec(diffusivity.shape, lambda b: (0, 0)),
            pl.BlockSpec(
                (TURN_SPECIES, tiles, LANES), lambda b: (jnp.minimum(b, last), 0, 0)
            ),
            pl.BlockSpec((PACK_BOXES, SLOTS, SR, SP), lambda b: (b, 0, 0, 0)),
        ],
        out_specs=[
            pl.BlockSpec((8, LANES), lambda b: (0, 0)),
            pl.BlockSpec((SR, LANES), lambda b: (0, 0)),
            pl.BlockSpec(
                (TURN_SPECIES, tiles, LANES), lambda b: (jnp.minimum(b, last), 0, 0)
            ),
        ]
        + [
            pl.BlockSpec((PACK_BOXES, n, PACK, LANES), lambda b: (b, 0, 0, 0)) for _, n in CHUNKS
        ],
        out_shape=[
            jax.ShapeDtypeStruct((8, LANES), jnp.int32),
            jax.ShapeDtypeStruct((SR, LANES), jnp.float32),
            jax.ShapeDtypeStruct((S, tiles, LANES), jnp.float32),
        ]
        + [
            jax.ShapeDtypeStruct((boxes, n, PACK, LANES), jnp.bfloat16) for _, n in CHUNKS
        ],
        compiler_params=pltpu.CompilerParams(vmem_limit_bytes=WIDE_VMEM),
        name="pack_all",
    )(pattern, table, counts, diffusivity, cells, jacobian)


def unpack(packed_ref, item, dense_ref):
    half_rows = SR // 2
    dense_ref[:, 0:LANES] = packed_ref[item, pl.ds(0, SR), :]
    middle = packed_ref[item, pl.ds(SR, half_rows), :]
    edge = packed_ref[item, pl.ds(SR + half_rows, BL), :]
    high = pltpu.roll(middle, BL, 1)

    def put(row, rows, low, rest):
        dense_ref[pl.ds(row, rows), LANES:SP] = jnp.where(lane_iota(rows) < BL, low, rest)

    put(0, 64, middle[0:64], pltpu.roll(edge, 64, 1))
    shifted = pltpu.roll(edge, 32, 1)
    put(64, 48, middle[64:112], shifted[0:48])
    put(112, 16, high[0:16], shifted[48:64])
    put(128, 64, high[16:80], edge)
    put(192, 32, high[80:112], pltpu.roll(edge[0:32], 96, 1))


def solve_kernel(chunk, *refs):
    if chunk == 0:
        plan_ref, state_hbm, packed_hbm, out_hbm, rows_hbm, edge_ref = refs[:6]
        scratch = refs[6:]
    else:
        plan_ref, state_hbm, packed_hbm, second_hbm, _, _, edge_in = refs[:7]
        out_hbm, rows_hbm, edge_ref = refs[7:10]
        scratch = refs[10:]
    packed, state, outgoing, arrived, sent = scratch[:5]
    dense, right, left_over, mapped, guess, sums = (
        scratch[5 + GROUP * kind : 5 + GROUP * (kind + 1)] for kind in range(6)
    )
    tiles = state_hbm.shape[1]
    begun = plan_ref[3, 0]
    base = 0 if chunk == 0 else begun
    groups = (begun if chunk == 0 else tiles - begun) // GROUP

    def fetch(place, origin, at):
        return pltpu.make_async_copy(origin.at[at], packed.at[place], arrived.at[0, place])

    def fetch_state(place):
        tile = plan_ref[1, base + place]
        return pltpu.make_async_copy(
            state_hbm.at[:, tile, :], state.at[place, 0:S], arrived.at[1, place]
        )

    def start_fetch(place, carry):
        at = plan_ref[0, base + place]
        state[place, SR - 8 : SR, :] = jnp.zeros((8, LANES), jnp.float32)
        fetch_state(place).start()
        if chunk == 0:
            fetch(place, packed_hbm, at).start()
        else:
            early = packed_hbm.shape[0]

            @pl.when(at < early)
            def _():
                fetch(place, packed_hbm, at).start()

            @pl.when(at >= early)
            def _():
                fetch(place, second_hbm, at - early).start()

        return carry

    lax.fori_loop(0, groups * GROUP, start_fetch, 0)
    for member in range(GROUP):
        right[member][SR:SP, :] = jnp.zeros((SP - SR, SP), jnp.bfloat16)
    if chunk == 0:
        edge_ref[...] = jnp.zeros_like(edge_ref)
    else:
        edge_ref[...] = edge_in[...]
    edge_lane = lane_iota(SR) // 4

    def send(buffer, member, tile):
        return pltpu.make_async_copy(
            outgoing.at[buffer, member], out_hbm.at[tile], sent.at[buffer, member]
        )

    def send_row(buffer, member, tile):
        at = jnp.where(tile < 2, tile, tile - (tiles - 4))
        return pltpu.make_async_copy(
            outgoing.at[buffer, member], rows_hbm.at[at], sent.at[2 + buffer, member]
        )

    def is_row(tile):
        return (tile < 2) | (tile >= tiles - 2)

    def drain(group_no):
        for member in range(GROUP):
            tile = plan_ref[1, base + group_no * GROUP + member]
            send(group_no % 2, member, tile).wait()

            @pl.when(is_row(tile))
            def _():
                send_row(group_no % 2, member, tile).wait()

    def split(member, row, rows, remainder):
        high = remainder.astype(jnp.bfloat16)
        span = slice(row, row + rows)
        right[member][span, 0:LANES] = high
        right[member][span, LANES:SP] = (remainder - high.astype(jnp.float32)).astype(
            jnp.bfloat16
        )

    def multiply(member):
        return jnp.dot(
            dense[member][...], right[member][...], preferred_element_type=jnp.float32
        )

    def measure(member, product):
        above = jnp.zeros((8, LANES), jnp.float32)
        below = jnp.zeros((8, LANES), jnp.float32)
        for row in range(0, SR, 8):
            span = slice(row, row + 8)
            remainder = left_over[member][span, :]
            value = remainder - (product[span, 0:LANES] + product[span, LANES:SP])
            mapped[member][span, :] = value
            above = above + remainder * value
            below = below + value * value
        return above, below

    def move(member, above, below, active):
        above = jnp.sum(above, axis=0, keepdims=True)
        below = jnp.sum(below, axis=0, keepdims=True) + EPSILON
        step = jnp.where(active, above / below, 0.0)
        for row in range(0, SR, 16):
            span = slice(row, row + 16)
            remainder = left_over[member][span, :]
            guess[member][span, :] += step * remainder
            remainder = remainder - step * mapped[member][span, :]
            left_over[member][span, :] = remainder
            split(member, row, 16, remainder)

    def keep_sums(member, above, below):
        sums[member][0:8, :] = above
        sums[member][8:16, :] = below

    def one_group(group_no, carry):
        buffer = group_no % 2
        places = [group_no * GROUP + member for member in range(GROUP)]
        chosen = [plan_ref[1, base + place] for place in places]
        counts = [plan_ref[2, base + place] for place in places]

        for member in range(GROUP):
            fetch(places[member], packed_hbm, 0).wait()
            fetch_state(places[member]).wait()
        def begin(member):
            unpack(packed, places[member], dense[member])
            start_value = state[places[member]]
            right[member][0:SR, 0:LANES] = start_value.astype(jnp.bfloat16)
            guess[member][...] = start_value
            remainder = jnp.dot(
                dense[member][...],
                right[member][:, 0:LANES],
                preferred_element_type=jnp.float32,
            )
            left_over[member][...] = remainder
            split(member, 0, SR, remainder)

        half = GROUP // 2
        for member in range(half, GROUP):
            begin(member)
        for one, other in zip(range(half), range(half, GROUP)):
            begin(one)
            keep_sums(other, *measure(other, multiply(other)))

        def advance(turn_no, inner):
            for one, other in zip(range(half), range(half, GROUP)):
                product = multiply(one)
                move(other, sums[other][0:8, :], sums[other][8:16, :], turn_no < counts[other])
                next_product = multiply(other)
                move(one, *measure(one, product), turn_no < counts[one])
                keep_sums(other, *measure(other, next_product))
            return inner

        lax.fori_loop(0, functools.reduce(jnp.maximum, counts), advance, 0)

        @pl.when(group_no >= 2)
        def _():
            drain(group_no - 2)

        for member in range(GROUP):
            result = guess[member][...]
            outgoing[buffer, member] = result
            tile = chosen[member]
            edge_ref[...] = jnp.where(
                edge_lane == tile, pltpu.roll(result, (4 * tile + 2) % LANES, 1), edge_ref[...]
            )
            send(buffer, member, tile).start()

            @pl.when(is_row(tile))
            def _():
                send_row(buffer, member, tile).start()

        return carry

    lax.fori_loop(0, groups, one_group, 0)

    for back in range(2):
        @pl.when(groups > back)
        def _():
            drain(groups - 1 - back)

    edge_ref[S + 2 : SR, :] = jnp.ones((SR - S - 2, LANES), jnp.float32)


def solve_chunk(chunk, plan, state, packed, reacted, rows, edge):
    tiles = state.shape[1]
    out_shape = (
        jax.ShapeDtypeStruct((tiles, SR, LANES), jnp.float32),
        jax.ShapeDtypeStruct((4, SR, LANES), jnp.float32),
        jax.ShapeDtypeStruct((SR, LANES), jnp.float32),
    )
    anywhere = pl.BlockSpec(memory_space=pl.ANY)
    vmem = pl.BlockSpec(memory_space=pltpu.VMEM)
    in_specs = [pl.BlockSpec(memory_space=pltpu.SMEM), anywhere]
    in_specs += [anywhere] * (chunk + 1)
    operands = [plan, state, *packed[: chunk + 1]]
    aliases = {}
    if chunk:
        in_specs += [anywhere, anywhere, vmem]
        operands += [reacted, rows, edge]
        aliases = {4: 0, 5: 1}
    tile_values = pltpu.VMEM((SR, LANES), jnp.float32)
    return pl.pallas_call(
        functools.partial(solve_kernel, chunk),
        in_specs=in_specs,
        out_specs=(anywhere, anywhere, vmem),
        out_shape=out_shape,
        input_output_aliases=aliases,
        scratch_shapes=[
            pltpu.VMEM((tiles, PACK, LANES), jnp.bfloat16),
            pltpu.VMEM((tiles, SR, LANES), jnp.float32),
            pltpu.VMEM((2, GROUP, SR, LANES), jnp.float32),
            pltpu.SemaphoreType.DMA((2, tiles)),
            pltpu.SemaphoreType.DMA((4, GROUP)),
        ]
        + [pltpu.VMEM((SR, SP), jnp.bfloat16)] * GROUP
        + [pltpu.VMEM((SP, SP), jnp.bfloat16)] * GROUP
        + [tile_values] * (3 * GROUP)
        + [pltpu.VMEM((16, LANES), jnp.float32)] * GROUP,
        compiler_params=pltpu.CompilerParams(vmem_limit_bytes=WIDE_VMEM),
        cost_estimate=pl.CostEstimate(
            flops=16 * 300_000_000, bytes_accessed=16 * 200000, transcendentals=0
        ),
        name="solve_chunk",
    )(*operands)


def is_odd(axis):
    return lax.rem(lax.axis_index(axis), 2) == 1


def message_kernel(rows_ref, near_ref, far_ref, near_out_ref, far_out_ref):
    tiles = LANES // 4
    lanes = lane_iota(SR)
    odd = is_odd("bal")
    low = jnp.where(odd, near_ref[...], far_ref[...])
    high = jnp.where(odd, far_ref[...], near_ref[...])
    odd = is_odd("box")

    def message(start, row, near):
        for to_near, out_ref in ((near, near_out_ref), (jnp.logical_not(near), far_out_ref)):

            @pl.when(to_near)
            def _():
                out_ref[0:2] = rows_ref[start : start + 2]
                cells = jnp.where(
                    lanes == 0,
                    pltpu.roll(low, (-(4 * row + 1)) % LANES, 1),
                    pltpu.roll(high, (-(4 * row + 3)) % LANES, 1),
                )
                out_ref[2] = jnp.where(lanes == 2, 1.0, cells).astype(jnp.bfloat16)

    message(0, 0, odd)
    message(2, tiles - 1, jnp.logical_not(odd))


def make_messages(rows, near, far):
    vmem = pl.BlockSpec(memory_space=pltpu.VMEM)
    shape = jax.ShapeDtypeStruct((3, SR, LANES), jnp.bfloat16)
    return pl.pallas_call(
        message_kernel,
        in_specs=[vmem, vmem, vmem],
        out_specs=(vmem, vmem),
        out_shape=(shape, shape),
        compiler_params=pltpu.CompilerParams(vmem_limit_bytes=TIGHT_VMEM),
        name="make_messages",
    )(rows, near, far)


def beside(value, lanes):
    return jnp.where(lanes == 0, 0.0, pltpu.roll(value, 1, 1)) + jnp.where(
        lanes == LANES - 1, 0.0, pltpu.roll(value, LANES - 1, 1)
    )


def inner_kernel(tiles, block_hbm, rate_ref, both_ref, out_ref, block_ref, arrived):
    zero = jnp.zeros((1, 8, LANES), jnp.float32)
    copies = [
        pltpu.make_async_copy(
            block_hbm.at[:, at : at + SPECIES, :], block_ref.at[:, at : at + SPECIES, :], arrived.at[k]
        )
        for k, at in enumerate(range(0, SR, SPECIES))
    ]
    for copy in copies:
        copy.start()

    def around(value, by):
        gap = jnp.concatenate([zero] * by, axis=0)
        return jnp.concatenate([gap, value[: tiles - by]], axis=0) + jnp.concatenate(
            [value[by:], gap], axis=0
        )

    for number in range(SR // 8):
        if number * 8 % SPECIES == 0:
            copies[number * 8 // SPECIES].wait()
        span = slice(number * 8, number * 8 + 8)
        rate = rate_ref[span, :]
        keep = 1.0 - 4.0 * rate
        square = rate * rate
        cells = block_ref[:, span, :]
        flat = cells.reshape(tiles * 8, LANES)
        high = flat.astype(jnp.bfloat16)
        low = (flat - high.astype(jnp.float32)).astype(jnp.bfloat16)
        product = jnp.dot(
            jnp.concatenate([high, low], axis=1), both_ref[...], preferred_element_type=jnp.float32
        )
        once = product[:, 0:LANES].reshape(tiles, 8, LANES)
        twice = product[:, LANES:].reshape(tiles, 8, LANES)
        near = (2.0 * keep * rate) * (around(cells, 1) + once)
        sides = around(once, 1)
        far = square * ((around(cells, 2) + twice) + (sides + sides))
        own = keep * keep + 2.0 * square
        end = keep * keep + square
        value = near + far
        out_ref[1 : tiles - 1, span, :] = value[1 : tiles - 1] + own * cells[1 : tiles - 1]
        out_ref[0, span, :] = value[0] + end * cells[0]
        out_ref[tiles - 1, span, :] = value[tiles - 1] + end * cells[tiles - 1]


def diffuse_inside(block, rate):
    tiles = block.shape[0]
    vmem = pl.BlockSpec(memory_space=pltpu.VMEM)
    place = np.arange(LANES)
    next_to = (np.abs(place[:, None] - place[None, :]) == 1).astype(np.float32)
    both = np.concatenate([next_to, next_to @ next_to], axis=1)
    both = jnp.asarray(np.concatenate([both, both], axis=0), jnp.bfloat16)
    return pl.pallas_call(
        functools.partial(inner_kernel, tiles),
        in_specs=[pl.BlockSpec(memory_space=pl.ANY), vmem, vmem],
        out_specs=vmem,
        out_shape=jax.ShapeDtypeStruct(block.shape, jnp.float32),
        scratch_shapes=[
            pltpu.VMEM(block.shape, jnp.float32),
            pltpu.SemaphoreType.DMA((SR // SPECIES,)),
        ],
        compiler_params=pltpu.CompilerParams(vmem_limit_bytes=INNER_VMEM),
        cost_estimate=pl.CostEstimate(
            flops=tiles * SR * LANES * 20, bytes_accessed=8 * block.size, transcendentals=0
        ),
        name="diffuse_inside",
    )(block, rate, both)


def border_kernel(tiles, inner_ref, top_ref, bottom_ref, near_row_ref, far_row_ref, near_ref,
                  far_ref, near_here_ref, far_here_ref, own_ref, rate_ref, out_ref):
    lanes = lane_iota(8)
    column = lanes % 4
    here = S + 2 - (SR - 8)
    from_near = (column < 2) == is_odd("bal")
    near_above = is_odd("box")
    has_side = jnp.where(
        from_near, near_here_ref[here : here + 1, :], far_here_ref[here : here + 1, :]
    )
    near_edge = (lanes < 2) | (lanes >= LANES - 2)

    def slab(number):
        span = slice(number * 8, number * 8 + 8)
        overall = pl.program_id(0) * (SPECIES // 8) + number
        wide = pl.ds(pl.multiple_of(overall // 2 * 16, 16), 16)

        def read(ref, row):
            both = ref[row, wide, :].astype(jnp.float32)
            return jnp.where(overall % 2 == 0, both[0:8], both[8:16])

        near_rows = [read(near_row_ref, row) for row in range(3)]
        far_rows = [read(far_row_ref, row) for row in range(3)]
        above = [jnp.where(near_above, a, b) for a, b in zip(near_rows, far_rows)]
        below = [jnp.where(near_above, b, a) for a, b in zip(near_rows, far_rows)]

        rate = rate_ref[span, :]
        keep = 1.0 - 4.0 * rate
        own = own_ref[span, :]
        ghost = jnp.where(from_near, near_ref[span, :], far_ref[span, :])

        def rows_beside(near, far, inner, corner):
            exists = jnp.broadcast_to(corner[:, 2:3], (8, LANES))
            left = jnp.where(lanes == 0, corner, pltpu.roll(near, 1, 1))
            right = jnp.where(lanes == LANES - 1, corner, pltpu.roll(near, LANES - 1, 1))
            later = (keep * near + rate * ((far + inner) + (left + right))) * exists
            first = rate * near
            outer = keep * first + rate * (beside(first, lanes) + later)
            return outer, rate * first

        corner_above, corner_below = above[2], below[2]
        row_terms = {}
        row_terms[0], row_terms[1] = rows_beside(
            above[1], above[0], top_ref[0, span, :], corner_above
        )
        row_terms[tiles - 1], row_terms[tiles - 2] = rows_beside(
            below[0], below[1], bottom_ref[0, span, :], corner_below
        )

        up = pltpu.roll(ghost, 4, 1)
        up = jnp.where(lanes == 1, pltpu.roll(corner_above, 1, 1), up)
        up = jnp.where(lanes == 2, pltpu.roll(corner_above, 3, 1), up)
        down = pltpu.roll(ghost, LANES - 4, 1)
        down = jnp.where(lanes == LANES - 3, pltpu.roll(corner_below, LANES - 3, 1), down)
        down = jnp.where(lanes == LANES - 2, pltpu.roll(corner_below, LANES - 1, 1), down)
        side = jnp.where(
            column == 1,
            pltpu.roll(own, LANES - 1, 1) + pltpu.roll(ghost, 1, 1),
            pltpu.roll(own, 1, 1) + pltpu.roll(ghost, LANES - 1, 1),
        )
        later = (keep * ghost + rate * ((up + down) + side)) * has_side
        first = rate * ghost
        first_up = jnp.where(lanes < 4, 0.0, pltpu.roll(first, 4, 1))
        first_down = jnp.where(lanes >= LANES - 4, 0.0, pltpu.roll(first, LANES - 4, 1))
        outer = keep * first + rate * ((first_up + first_down) + later)
        second = rate * first
        terms = jnp.where(
            column < 2,
            jnp.where(column == 0, pltpu.roll(second, LANES - 2, 1), pltpu.roll(outer, LANES - 1, 1)),
            jnp.where(column == 2, pltpu.roll(outer, 1, 1), pltpu.roll(second, 2, 1)),
        )
        values = []
        for row in range(tiles):
            value = inner_ref[row, span, :] + jnp.where(
                near_edge, pltpu.roll(terms, (-(4 * row + 2)) % LANES, 1), 0.0
            )
            if row in row_terms:
                value = value + row_terms[row]
            values.append(value)
        out_ref[span, :, :] = jnp.swapaxes(jnp.stack(values, axis=0), 0, 1)

    for number in range(SPECIES // 8):
        slab(number)


def add_borders(inner, rows, near_row, far_row, near, far, own, rate):
    tiles = inner.shape[0]
    message = pl.BlockSpec((3, SR, LANES), lambda g: (0, 0, 0))
    edge = pl.BlockSpec((SPECIES, LANES), lambda g: (g, 0))
    flags = pl.BlockSpec((8, LANES), lambda g: (SR // 8 - 1, 0))
    return pl.pallas_call(
        functools.partial(border_kernel, tiles),
        grid=(SR // SPECIES,),
        in_specs=[
            pl.BlockSpec((tiles, SPECIES, LANES), lambda g: (0, g, 0)),
            pl.BlockSpec((1, SPECIES, LANES), lambda g: (0, g, 0)),
            pl.BlockSpec((1, SPECIES, LANES), lambda g: (3, g, 0)),
            message,
            message,
            edge,
            edge,
            flags,
            flags,
            edge,
            edge,
        ],
        out_specs=pl.BlockSpec((SPECIES, tiles, LANES), lambda g: (g, 0, 0)),
        out_shape=jax.ShapeDtypeStruct((S, tiles, LANES), jnp.float32),
        compiler_params=pltpu.CompilerParams(vmem_limit_bytes=TIGHT_VMEM),
        name="add_borders",
    )(inner, rows, rows, near_row, far_row, near, far, near, far, own, rate)


def trade(near_value, far_value, axis):
    count = lax.axis_size(axis)
    near = [(i, i ^ 1) for i in range(count) if i ^ 1 < count]
    far = [(i, j) for i in range(count) for j in [i + 1 if i % 2 else i - 1] if 0 <= j < count]
    return lax.ppermute(near_value, axis, near), lax.ppermute(far_value, axis, far)


def on_device(species_state, stiffness, send_list, jacobian, pattern, diffusivity):
    boxes = lax.axis_size("box")
    tiles = species_state.shape[0]
    slots = jacobian.shape[0] // boxes
    by_box = jacobian.reshape(boxes, slots, SP, SP)
    counts = stiffness.reshape(1, tiles)
    table = send_list.transpose(0, 1, 3, 2).reshape(slots, boxes)
    by_block = pattern.transpose(1, 2, 3, 0).reshape(NB, NB, boxes * slots)
    plan, rate, state, first, second = pack_all(
        by_box, by_block, table, counts, diffusivity.reshape(1, S), species_state.transpose(1, 0, 2)
    )
    plan, rate, state, first, second = lax.optimization_barrier(
        (plan, rate, state, first, second)
    )

    def exchange(packed):
        arrived = lax.all_to_all(packed, "box", split_axis=0, concat_axis=0, tiled=True)
        return arrived.reshape(-1, PACK, LANES)

    first = exchange(first)
    plan, rate, state, first, second = lax.optimization_barrier(
        (plan, rate, state, first, second)
    )
    second = exchange(second)
    early, rows, edge = solve_chunk(0, plan, state, (first, second), None, None, None)
    reacted, rows, edge = solve_chunk(1, plan, state, (first, second), early, rows, edge)

    near, far = trade(edge, edge, "bal")
    messages = make_messages(rows.astype(jnp.bfloat16), near, far)
    near_row, far_row = trade(*messages, "box")
    inner = diffuse_inside(reacted, rate)
    field = add_borders(inner, rows, near_row, far_row, near, far, edge, rate)
    return field.transpose(1, 0, 2)


def solution(mesh):
    in_specs = (
        P("box", None, "bal"),
        P("box", "bal"),
        P("box", "bal", None, None),
        P("box", "bal", None, None),
        P("box", "bal", None, None),
        P(),
    )
    return jax.shard_map(
        on_device,
        mesh=mesh,
        in_specs=in_specs,
        out_specs=P("box", None, "bal"),
        check_vma=False,
    )
```
